256 devices in a mesh: dp: 32 (over y, z), tensor: 8 (over x, core).
Axes of the slice: x: 4, y: 4, z: 8, core: 2. Of those that a mesh axis runs over, the one named last changes fastest.
Arguments:
- queries: bfloat16 [16384, 8192], P('dp', 'tensor'), may hold values from -140 to 140
- keys: bfloat16 [16384, 1024], P('dp', 'tensor'), may hold values from -6 to 6
- values: bfloat16 [16384, 1024], P('dp', 'tensor'), may hold values from -6 to 6
- out_grad: bfloat16 [16384, 3072], P('dp', 'tensor'), may hold values from -6 to 6
- out_weight: bfloat16 [8192, 3072], P('tensor'), may hold values from -0.109375 to 0.109375
- send_slot: int32 [16384], P('dp'), may hold values from 0 to 1023, as said below
- recv_index: int32 [16384], P('dp'), may hold values from 0 to 1023, as said below
- packed_doc: int32 [16384], P('dp'), may hold values from 0 to 127, as said below
Outputs:
- query_grad: bfloat16 [16384, 8192], P('dp', 'tensor')
- key_grad: bfloat16 [16384, 1024], P('dp', 'tensor')
- value_grad: bfloat16 [16384, 1024], P('dp', 'tensor')
- weight_grad: float32 [3072, 8192], P('dp', 'tensor')
The draws below stay inside these ranges and needn't reach their ends.
Inputs may be any that keep to these rules, and one draw needn't show every extreme that they name: `send_slot`: for the 512 tokens of one index of dp the values are distinct; a value s sends the token to index s // 32 of dp, into place s % 32 among the tokens sent there. The places used from one index toward one index are 0, 1, ... without gaps, at most 32 of them, and every index receives exactly 512 tokens. `recv_index`: on each index of dp the 512 values are distinct and name exactly the received places that were filled, as source * 32 + place, sources increasing and places increasing within a source; entry i gives packed row i. `packed_doc`: on each index of dp the document number starts at 0 and rises by 0 or 1 from one packed row to the next.
All inputs are finite; a program needn't handle non-finite values.
Results may differ from the reference program's by a relative error of at most 0.02.
Values may be sent and summed in bfloat16 or wider, within the bound.
A program may use at most 128 MiB of HBM per device.

```python
import math
import jax
import jax.numpy as jnp
from jax import lax

D = 3072
HEADS = 64
KV_HEADS = 8
HEAD_DIM = 128
TOK_DEV = 512
TOKENS = 16384
CAP = 32
N_DP = 32


def plan_tables(key):
    key = jax.random.fold_in(key, 71)
    key_a, key_b, key_c, key_d, key_e, key_f, key_g = jax.random.split(key, 7)
    even_share = TOK_DEV // N_DP
    upper_half = jax.random.randint(key_a, (N_DP // 2,), 0, even_share + 1).at[0].set(even_share)
    offsets = jnp.concatenate([upper_half, -upper_half])
    column_order = jax.random.permutation(key_b, N_DP)
    row_order = jax.random.permutation(key_c, N_DP)
    counts = even_share + offsets[(column_order[None, :] - row_order[:, None]) % N_DP]
    slot_lane = jnp.arange(CAP)
    live_slots = slot_lane[None, None, :] < counts[:, :, None]
    send_order = jnp.argsort(jnp.where(live_slots.reshape(N_DP, N_DP * CAP), 0, 1), axis=1, stable=True)[:, :TOK_DEV].astype(jnp.int32)
    shuffle = jax.vmap(lambda part_key: jax.random.permutation(part_key, TOK_DEV))(jax.random.split(key_d, N_DP))
    rank_ids = jnp.arange(N_DP)[:, None]
    send_table = jnp.zeros((N_DP, TOK_DEV), jnp.int32).at[rank_ids, shuffle].set(send_order)
    arrive_slots = jnp.swapaxes(live_slots, 0, 1).reshape(N_DP, N_DP * CAP)
    recv_table = jnp.argsort(jnp.where(arrive_slots, 0, 1), axis=1, stable=True)[:, :TOK_DEV].astype(jnp.int32)
    positions = jnp.broadcast_to(jnp.arange(TOK_DEV, dtype=jnp.int32), (N_DP, TOK_DEV))
    owner_table = jnp.zeros((N_DP, N_DP * CAP), jnp.int32).at[rank_ids, send_table].set(positions)
    sender_rank = recv_table // CAP
    anchor_rows = sender_rank * TOK_DEV + owner_table[sender_rank, rank_ids * CAP + recv_table % CAP]
    doc_spans = jax.random.randint(key_e, (N_DP, 1), 3, 10)
    coin_flips = jax.random.randint(key_f, (N_DP, TOK_DEV), 0, 1 << 20)
    busy_rank = jax.random.randint(key_g, (), 0, N_DP)
    row_places = jnp.arange(TOK_DEV)[None, :]
    forced = (jnp.arange(N_DP)[:, None] == busy_rank) & (row_places % 4 == 0)
    doc_starts = ((coin_flips < jnp.right_shift(jnp.int32(1 << 20), doc_spans)) | forced) & (row_places > 0)
    documents = jnp.minimum(jnp.cumsum(doc_starts.astype(jnp.int32), axis=1), TOK_DEV // 4 - 1).astype(jnp.int32)
    return (send_table, recv_table, anchor_rows, documents)


def attention_fields(key, picks):
    tables = plan_tables(key)
    anchor_rows = tables[2]
    documents = tables[3]
    key = jax.random.fold_in(key, 29)
    key_a, key_b, key_c = jax.random.split(key, 3)
    key_field = jnp.clip(jax.random.normal(key_a, (TOKENS, KV_HEADS * HEAD_DIM), jnp.float32), -6.0, 6.0)
    query_field = jnp.clip(jax.random.normal(key_b, (TOKENS, HEADS * HEAD_DIM), jnp.float32), -6.0, 6.0)
    rank_ids = jnp.arange(N_DP)[:, None]
    spots = jax.random.randint(key_c, (N_DP, picks), 1, TOK_DEV)
    joined = documents[rank_ids, spots] == documents[rank_ids, spots - 1]
    target = jnp.where(joined, anchor_rows[rank_ids, spots], TOKENS).reshape(-1)
    earlier = jnp.where(joined, anchor_rows[rank_ids, spots - 1], TOKENS).reshape(-1)
    strength = 14.0 + 4.0 * (jnp.arange(N_DP * picks) % 3).astype(jnp.float32)
    chosen = key_field[jnp.minimum(target, TOKENS - 1)]
    shrink = 1.0 - 2.0 / (strength * math.sqrt(HEAD_DIM))
    key_field = key_field.at[earlier].set(shrink[:, None] * chosen, mode='drop')
    group = HEADS // KV_HEADS
    lifted = strength[:, None, None, None] * chosen.reshape(-1, KV_HEADS, 1, HEAD_DIM)
    lifted = jnp.broadcast_to(lifted, (lifted.shape[0], KV_HEADS, group, HEAD_DIM)).reshape(-1, HEADS * HEAD_DIM)
    query_field = query_field.at[target].set(lifted, mode='drop')
    return (query_field, key_field)


def draw_queries(key, part):
    picks = 0
    return attention_fields(key, picks)[0].astype(jnp.bfloat16)


def draw_keys(key, part):
    picks = 0
    return attention_fields(key, picks)[1].astype(jnp.bfloat16)


def draw_send_slot(key, part):
    return plan_tables(key)[0].reshape(TOKENS)


def draw_recv_index(key, part):
    return plan_tables(key)[1].reshape(TOKENS)


def draw_packed_doc(key, part):
    return plan_tables(key)[3].reshape(TOKENS)


def strengthened(result, key, source, target, shards_of, factor):
    def block_of(position):
        return (jnp.arange(result.shape[position]) // (result.shape[position] // shards_of)).reshape((-1,) + (1,) * (result.ndim - 1 - position))

    one_side = jax.random.permutation(key, shards_of)[block_of(target)]
    second = (block_of(target) + shards_of // 2) % shards_of
    return jnp.where((block_of(source) == one_side) | (block_of(source) == second), factor * result, result)


def block_levels(rng, dims, pieces, low, high):
    def one(position, shards_of):
        heights = jax.random.uniform(jax.random.fold_in(jax.random.fold_in(rng, 6), position), (shards_of,), jnp.float32, low / len(pieces), high / len(pieces))
        return jnp.repeat(jnp.exp(heights), dims[position] // shards_of).reshape((-1,) + (1,) * (len(dims) - position - 1))

    level = one(*pieces[0])
    for cut in pieces[1:]:
        level = level * one(*cut)
    return level


def normal_values(key, extent, width, limit, shards=(), kind=jnp.bfloat16):
    entries = jax.random.normal(key, extent, jnp.float32) * width
    if len(shards) > 0:
        entries = block_levels(key, extent, shards, -0.22, 0.18) * entries
    return jnp.clip(entries, min=-limit, max=limit).astype(kind)


def gaussian_with(stream_key, extent, spread, reach, shards, heavy, kind=jnp.bfloat16):
    drawn = spread * jax.random.normal(stream_key, extent, jnp.float32)
    if shards:
        drawn = drawn * block_levels(stream_key, extent, shards, -0.22, 0.18)
    return jnp.clip(strengthened(drawn, jax.random.fold_in(stream_key, 3), *heavy), -reach, reach).astype(kind)


def setup_inputs(seed: int = 0) -> dict:
    arg_keys = jax.random.split(jax.random.key(seed), 9)
    return {
        "queries": draw_queries(jax.random.fold_in(arg_keys[8], 71), 0),
        "keys": draw_keys(jax.random.fold_in(arg_keys[8], 71), 0),
        "values": normal_values(arg_keys[2], (TOKENS, KV_HEADS * HEAD_DIM), 1.0, 6.0, ((0, 32), (1, 8))),
        "out_grad": gaussian_with(arg_keys[3], (TOKENS, D), 1.0, 6.0, ((0, 32), (1, 8)), (0, 1, 32, 2.75)),
        "out_weight": normal_values(arg_keys[4], (HEADS * HEAD_DIM, D), D ** -0.5, 0.109375, ((0, 8),)),
        "send_slot": draw_send_slot(jax.random.fold_in(arg_keys[8], 71), 0),
        "recv_index": draw_recv_index(jax.random.fold_in(arg_keys[8], 71), 0),
        "packed_doc": draw_packed_doc(jax.random.fold_in(arg_keys[8], 71), 0),
    }


def source_rows(send_slot, recv_index):
    lanes = N_DP * CAP
    anchor = jnp.arange(TOKENS, dtype=jnp.int32)
    owner_rank = anchor // TOK_DEV
    target = send_slot // CAP * lanes + owner_rank * CAP + send_slot % CAP
    table = jnp.zeros((N_DP * lanes,), jnp.int32).at[target.astype(jnp.int32)].set(anchor)
    return table[(owner_rank * lanes + recv_index).astype(jnp.int32)]

def attention_backward(query_pack, key_pack, value_pack, head_grad, doc_rank):
    tok_rows = query_pack.shape[0]
    kv_local = key_pack.shape[1] // HEAD_DIM
    group = HEADS // KV_HEADS
    inv_root = 1.0 / math.sqrt(HEAD_DIM)
    query_heads = query_pack.reshape(tok_rows, kv_local, group, HEAD_DIM).astype(jnp.float32)
    key_heads = key_pack.reshape(tok_rows, kv_local, HEAD_DIM).astype(jnp.float32)
    value_heads = value_pack.reshape(tok_rows, kv_local, HEAD_DIM).astype(jnp.float32)
    grad_heads = head_grad.reshape(tok_rows, kv_local, group, HEAD_DIM).astype(jnp.float32)
    scores = jnp.einsum('tkgd,skd->kgts', query_heads, key_heads) * inv_root
    places = jnp.arange(tok_rows, dtype=jnp.int32)
    visible = (doc_rank[:, None] == doc_rank[None, :]) & (places[None, :] <= places[:, None])
    scores = jnp.where(visible, scores, -1e+30)
    row_top = lax.optimization_barrier(jnp.max(scores, axis=-1, keepdims=True))
    raised = jnp.exp(scores - row_top)
    soft = raised / lax.optimization_barrier(jnp.sum(raised, axis=-1, keepdims=True))
    soft_half = soft.astype(jnp.bfloat16)
    attended = jnp.einsum('kgts,skd->tkgd', soft_half.astype(jnp.float32), value_heads)
    attended = attended.astype(jnp.bfloat16).reshape(tok_rows, -1)
    soft_grad = jnp.einsum('tkgd,skd->kgts', grad_heads, value_heads)
    inner = lax.optimization_barrier(jnp.sum(soft * soft_grad, axis=-1, keepdims=True))
    score_grad = (soft * (soft_grad - inner)).astype(jnp.bfloat16).astype(jnp.float32)
    query_delta = (jnp.einsum('kgts,skd->tkgd', score_grad, key_heads) * inv_root).astype(jnp.bfloat16)
    key_delta = (jnp.einsum('kgts,tkgd->skd', score_grad, query_heads) * inv_root).astype(jnp.bfloat16)
    value_delta = jnp.einsum('kgts,tkgd->skd', soft_half.astype(jnp.float32), grad_heads).astype(jnp.bfloat16)
    return (attended, query_delta.reshape(tok_rows, -1), key_delta.reshape(tok_rows, -1), value_delta.reshape(tok_rows, -1))

def reference(queries, keys, values, out_grad, out_weight, send_slot, recv_index, packed_doc):
    source = source_rows(send_slot, recv_index)
    norm_scale = 1.0 / math.sqrt(TOKENS)
    stacked = (queries[source].reshape(N_DP, TOK_DEV, HEADS * HEAD_DIM), keys[source].reshape(N_DP, TOK_DEV, KV_HEADS * HEAD_DIM), values[source].reshape(N_DP, TOK_DEV, KV_HEADS * HEAD_DIM), out_grad[source].reshape(N_DP, TOK_DEV, D), packed_doc.reshape(N_DP, TOK_DEV))

    def per_rank(total, slabs):
        query_pack, key_pack, value_pack, grad_full, doc_rank = slabs
        head_grad = lax.dot_general(grad_full, out_weight, (((1,), (1,)), ((), ())), preferred_element_type=jnp.float32).astype(jnp.bfloat16)
        attended, query_delta, key_delta, value_delta = attention_backward(query_pack, key_pack, value_pack, head_grad, doc_rank)
        partial_term = lax.dot_general(grad_full, attended, (((0,), (0,)), ((), ())), preferred_element_type=jnp.float32) * norm_scale
        partial_term = lax.optimization_barrier(partial_term.astype(jnp.bfloat16))
        return (total + partial_term.astype(jnp.float32), (query_delta, key_delta, value_delta))
    weight_grad, deltas = lax.scan(per_rank, jnp.zeros((D, HEADS * HEAD_DIM), jnp.float32), stacked)
    query_grad = jnp.zeros((TOKENS, HEADS * HEAD_DIM), deltas[0].dtype).at[source].set(deltas[0].reshape(TOKENS, -1))
    key_grad = jnp.zeros((TOKENS, KV_HEADS * HEAD_DIM), deltas[1].dtype).at[source].set(deltas[1].reshape(TOKENS, -1))
    value_grad = jnp.zeros((TOKENS, KV_HEADS * HEAD_DIM), deltas[2].dtype).at[source].set(deltas[2].reshape(TOKENS, -1))
    return (query_grad, key_grad, value_grad, weight_grad)
```

```python
import functools
import math

import jax
import jax.numpy as jnp
from jax import lax
from jax.experimental import pallas as pl
from jax.experimental.pallas import tpu as pltpu
from jax.sharding import PartitionSpec as P

HEADS = 64
KV_HEADS = 8
HEAD_DIM = 128
MESH = pl.DeviceIdType.MESH


def attention_backward(query_pack, key_pack, value_pack, head_grad, doc_rank):
    tok_rows = query_pack.shape[0]
    kv_local = key_pack.shape[1] // HEAD_DIM
    group = HEADS // KV_HEADS
    inv_root = 1.0 / math.sqrt(HEAD_DIM)
    query_heads = query_pack.reshape(tok_rows, kv_local, group, HEAD_DIM)
    key_heads = key_pack.reshape(tok_rows, kv_local, HEAD_DIM)
    value_heads = value_pack.reshape(tok_rows, kv_local, HEAD_DIM)
    grad_heads = head_grad.reshape(tok_rows, kv_local, group, HEAD_DIM)
    scores = (
        jnp.einsum("tkgd,skd->kgts", query_heads, key_heads, preferred_element_type=jnp.float32)
        * inv_root
    )
    places = jnp.arange(tok_rows, dtype=jnp.int32)
    visible = (doc_rank[:, None] == doc_rank[None, :]) & (places[None, :] <= places[:, None])
    scores = jnp.where(visible, scores, -1e30)
    row_top = jnp.max(scores, axis=-1, keepdims=True)
    raised = jnp.exp(scores - row_top)
    soft = raised / jnp.sum(raised, axis=-1, keepdims=True)
    soft_half = soft.astype(jnp.bfloat16)
    attended = jnp.einsum(
        "kgts,skd->tkgd", soft_half, value_heads, preferred_element_type=jnp.float32
    )
    attended = attended.astype(jnp.bfloat16).reshape(tok_rows, -1)
    soft_grad = jnp.einsum(
        "tkgd,skd->kgts", grad_heads, value_heads, preferred_element_type=jnp.float32
    )
    inner = jnp.sum(soft * soft_grad, axis=-1, keepdims=True)
    score_grad = (soft * (soft_grad - inner)).astype(jnp.bfloat16)
    query_delta = (
        jnp.einsum("kgts,skd->tkgd", score_grad, key_heads, preferred_element_type=jnp.float32)
        * inv_root
    ).astype(jnp.bfloat16)
    key_delta = (
        jnp.einsum("kgts,tkgd->skd", score_grad, query_heads, preferred_element_type=jnp.float32)
        * inv_root
    ).astype(jnp.bfloat16)
    value_delta = jnp.einsum(
        "kgts,tkgd->skd", soft_half, grad_heads, preferred_element_type=jnp.float32
    ).astype(jnp.bfloat16)
    return (
        attended,
        query_delta.reshape(tok_rows, -1),
        key_delta.reshape(tok_rows, -1),
        value_delta.reshape(tok_rows, -1),
    )


def rs_kernel(ny, nz, w_ref, out_ref, za, zb, ya, yb, zs, zr, ys, yr):
    me = lax.axis_index("dp")
    my_y, my_z = me // nz, lax.rem(me, nz)
    def at(y, z):
        return lax.rem(y + 2 * ny, ny) * nz + lax.rem(z + 2 * nz, nz)
    sem = pltpu.get_barrier_semaphore()
    for n in (at(my_y, my_z + 1), at(my_y, my_z - 1), at(my_y + 1, my_z), at(my_y - 1, my_z)):
        pl.semaphore_signal(sem, inc=1, device_id={"dp": n}, device_id_type=MESH)
    pl.semaphore_wait(sem, 4)

    cols = w_ref.shape[-1]
    f32 = jnp.float32

    def zid(k):
        return lax.rem(my_z + 2 * nz + k, nz)

    def yid(k):
        return lax.rem(my_y + 2 * ny + k, ny)

    def send(src, dst, ss, rs, dev):
        c = pltpu.make_async_remote_copy(src_ref=src, dst_ref=dst, send_sem=ss, recv_sem=rs,
                                         device_id={"dp": dev}, device_id_type=MESH)
        c.start()
        return c

    zdev = [at(my_y, my_z + 1), at(my_y, my_z - 1)]
    ydev = [at(my_y + 1, my_z), at(my_y - 1, my_z)]
    sign = [1, -1]
    cps = {}
    for i in range(2):
        g = sign[i]
        cps["ya", i, 0] = send(w_ref.at[2 + i, yid(-g)], ya.at[i, 0], ys.at[i, 0], yr.at[i, 0], ydev[i])
    for i in range(2):
        g = sign[i]
        for k in range(ny):
            pass
        cps["za", i, 0] = send(w_ref.at[i, :, zid(-g)], za.at[i, 0], zs.at[i, 0], zr.at[i, 0], zdev[i])
    allc = []

    def z_first(i, s):
        g = sign[i]
        cps["za", i, s].wait_recv()
        c = zid(-g * (2 + s))
        if s < nz - 2:
            za[i, s] = (za[i, s].astype(f32) + w_ref[i, :, c].astype(f32)).astype(jnp.bfloat16)
            cps["za", i, s + 1] = send(za.at[i, s], za.at[i, s + 1], zs.at[i, s + 1], zr.at[i, s + 1], zdev[i])
        else:
            za[i, s] = (za[i, s].astype(f32) + w_ref[i, :, c].astype(f32)).astype(jnp.bfloat16)
            cps["yb", i, 0] = send(za.at[i, s, yid(-g)], yb.at[i, 0], ys.at[i, ny - 1], yr.at[i, ny - 1], ydev[i])

    def y_second(i, s):
        g = sign[i]
        cps["yb", i, s].wait_recv()
        c = yid(-g * (2 + s))
        tot = yb[i, s].astype(f32) + za[i, nz - 2, c].astype(f32)
        if s < ny - 2:
            yb[i, s] = tot.astype(jnp.bfloat16)
            cps["yb", i, s + 1] = send(yb.at[i, s], yb.at[i, s + 1], ys.at[i, ny + s], yr.at[i, ny + s], ydev[i])
        else:
            out_ref[:, i * cols:(i + 1) * cols] = tot

    def y_first(i, s):
        g = sign[i]
        cps["ya", i, s].wait_recv()
        c = yid(-g * (2 + s))
        ya[i, s] = (ya[i, s].astype(f32) + w_ref[2 + i, c].astype(f32)).astype(jnp.bfloat16)
        if s < ny - 2:
            cps["ya", i, s + 1] = send(ya.at[i, s], ya.at[i, s + 1], ys.at[i, s + 1], yr.at[i, s + 1], ydev[i])
        else:
            cps["zb", i, 0] = send(ya.at[i, s, zid(-g)], zb.at[i, 0], zs.at[i, nz - 1], zr.at[i, nz - 1], zdev[i])

    def z_second(i, s):
        g = sign[i]
        cps["zb", i, s].wait_recv()
        c = zid(-g * (2 + s))
        tot = zb[i, s].astype(f32) + ya[i, ny - 2, c].astype(f32)
        if s < nz - 2:
            zb[i, s] = tot.astype(jnp.bfloat16)
            cps["zb", i, s + 1] = send(zb.at[i, s], zb.at[i, s + 1], zs.at[i, nz + s], zr.at[i, nz + s], zdev[i])
        else:
            out_ref[:, (2 + i) * cols:(3 + i) * cols] = tot

    order = []
    za_steps = [(z_first, s) for s in range(nz - 1)] + [(y_second, s) for s in range(ny - 1)]
    ya_steps = [(y_first, s) for s in range(ny - 1)] + [(z_second, s) for s in range(nz - 1)]
    ta = [(s + 1) * 4.0 for s in range(nz - 1)]
    ta += [ta[-1] + (s + 1) * 1.5 for s in range(ny - 1)]
    tb = [(s + 1) * 8.0 for s in range(ny - 1)]
    tb += [tb[-1] + (s + 1) * 1.5 for s in range(nz - 1)]
    plan = [(t, 0, f, s) for t, (f, s) in zip(ta, za_steps)] + [(t, 1, f, s) for t, (f, s) in zip(tb, ya_steps)]
    plan.sort(key=lambda e: (e[0], e[1]))
    for _, _, f, s in plan:
        for i in range(2):
            f(i, s)
    for c in cps.values():
        c.wait_send()

def reduce_scatter(w, ny, nz):
    _, _, _, rows, cols = w.shape
    return pl.pallas_call(
        functools.partial(rs_kernel, ny, nz),
        out_shape=jax.ShapeDtypeStruct((rows, 4 * cols), jnp.float32),
        in_specs=[pl.BlockSpec(memory_space=pltpu.VMEM)],
        out_specs=pl.BlockSpec(memory_space=pltpu.VMEM),
        scratch_shapes=[
            pltpu.VMEM((2, nz - 1, ny, rows, cols), jnp.bfloat16),
            pltpu.VMEM((2, nz - 1, rows, cols), jnp.bfloat16),
            pltpu.VMEM((2, ny - 1, nz, rows, cols), jnp.bfloat16),
            pltpu.VMEM((2, ny - 1, rows, cols), jnp.bfloat16),
            pltpu.SemaphoreType.DMA((2, 2 * (nz - 1))),
            pltpu.SemaphoreType.DMA((2, 2 * (nz - 1))),
            pltpu.SemaphoreType.DMA((2, 2 * (ny - 1))),
            pltpu.SemaphoreType.DMA((2, 2 * (ny - 1))),
        ],
        compiler_params=pltpu.CompilerParams(collective_id=1, has_side_effects=True, vmem_limit_bytes=48 << 20),
        name="weight_grad_rings",
    )(w)


def place_rows(onehot, rows):
    return lax.dot_general(
        onehot, rows, (((1,), (0,)), ((), ())), preferred_element_type=jnp.float32
    ).astype(jnp.bfloat16)


def take_rows(onehot, rows):
    return lax.dot_general(
        onehot, rows, (((0,), (0,)), ((), ())), preferred_element_type=jnp.float32
    ).astype(jnp.bfloat16)


def swap(rows):
    return lax.all_to_all(rows, "dp", split_axis=0, concat_axis=0, tiled=True)


def shards(ny, nz, queries, keys, values, out_grad, out_weight, send_slot, recv_index, packed_doc):
    tok_rows = queries.shape[0]
    peers = ny * nz
    lanes = 2 * tok_rows
    slots = lax.broadcasted_iota(jnp.int32, (lanes, tok_rows), 0)
    send_hot = (slots == send_slot[None, :]).astype(jnp.bfloat16)
    recv_hot = (slots == recv_index[None, :]).astype(jnp.bfloat16)
    grad_moved = swap(place_rows(send_hot, out_grad))
    qkv = place_rows(send_hot, jnp.concatenate([queries, keys, values], axis=1))
    qkv, grad_moved = lax.optimization_barrier((qkv, grad_moved))
    moved = swap(qkv)
    grad_part = take_rows(recv_hot, grad_moved)
    grad_full = lax.all_gather(grad_part, "tensor", axis=1, tiled=True)
    head_grad = lax.dot_general(
        grad_full, out_weight, (((1,), (1,)), ((), ())), preferred_element_type=jnp.float32
    ).astype(jnp.bfloat16)
    pack = take_rows(recv_hot, moved)
    width = queries.shape[1]
    kvw = keys.shape[1]
    attended, query_delta, key_delta, value_delta = attention_backward(
        pack[:, :width], pack[:, width:width + kvw], pack[:, width + kvw:], head_grad, packed_doc
    )
    norm_scale = 1.0 / math.sqrt(tok_rows * peers)
    part = jnp.einsum(
        "tf,tsc->sfc", grad_full, attended.reshape(tok_rows, 4, width // 4),
        preferred_element_type=jnp.float32,
    )
    part = (part * norm_scale).astype(jnp.bfloat16)
    feats = part.shape[1]
    part = part.reshape(4, ny, nz, feats // peers, width // 4)
    back = place_rows(recv_hot, jnp.concatenate([query_delta, key_delta, value_delta], axis=1))
    returned = swap(back)
    weight_grad = reduce_scatter(part, ny, nz)
    home = take_rows(send_hot, returned)
    return home[:, :width], home[:, width:width + kvw], home[:, width + kvw:], weight_grad


def solution(mesh):
    placed = (
        P("dp", "tensor"),
        P("dp", "tensor"),
        P("dp", "tensor"),
        P("dp", "tensor"),
        P("tensor", None),
        P("dp"),
        P("dp"),
        P("dp"),
    )
    nz = 8 if mesh.shape["dp"] % 8 == 0 else 1
    ny = mesh.shape["dp"] // nz
    return jax.shard_map(
        functools.partial(shards, ny, nz),
        mesh=mesh,
        in_specs=placed,
        out_specs=(P("dp", "tensor"), P("dp", "tensor"), P("dp", "tensor"), P("dp", "tensor")),
        check_vma=False,
    )
```

```python
import functools
import math

import jax
import jax.numpy as jnp
from jax import lax
from jax.experimental import pallas as pl
from jax.experimental.pallas import tpu as pltpu
from jax.sharding import PartitionSpec as P

MESH = pl.DeviceIdType.MESH
BF = jnp.bfloat16
F32 = jnp.float32
CAP = 32
HEAD_DIM = 128
NY = 4
NZ = 8
NX = 4
NDP = NY * NZ
TOK = 512
LANES = NDP * CAP
BLK = 256
NB = 4
PART = 384
FEAT = 3072
ROWS = FEAT // NDP
SLAB = NZ * ROWS


def nn(a, b):
    return lax.dot_general(a, b, (((1,), (0,)), ((), ())), preferred_element_type=F32)


def nt(a, b):
    return lax.dot_general(a, b, (((1,), (1,)), ((), ())), preferred_element_type=F32)


def kernel(
    q_ref, k_ref, v_ref, g_ref, w_ref, ss_row, ss_col, ri_row, ri_col, doc_row, doc_col,
    qg_ref, kg_ref, vg_ref, wg_ref,
    send_g, recv_g, send_x, recv_x, back, home,
    sel_r, sel_rt, gt, bias, kv, kvt, dkv, hgt, att, dqt,
    part, ya, yb, yc, yt, za, zb,
    sem_gs, sem_gr, sem_xs, sem_xr, sem_bs, sem_br, sem_as, sem_ar, sem_ys, sem_yr, sem_zs, sem_zr,
):
    me = lax.axis_index("dp")
    tp = lax.axis_index("tensor")
    my_y, my_z = me // NZ, lax.rem(me, NZ)
    my_x, core = tp // 2, lax.rem(tp, 2)

    def peer(k):
        return lax.rem(my_y + k // NZ, NY) * NZ + lax.rem(my_z + 3 * k, NZ)

    def x_dev(dx, c):
        return lax.rem(my_x + dx + NX, NX) * 2 + c

    def dp_dev(dy, dz):
        return lax.rem(my_y + dy + NY, NY) * NZ + lax.rem(my_z + dz + NZ, NZ)

    barrier = pltpu.get_barrier_semaphore()

    def greet(k, _):
        pl.semaphore_signal(barrier, inc=1, device_id={"dp": peer(k)}, device_id_type=MESH)
        return 0

    lax.fori_loop(1, NDP, greet, 0)
    for t in (x_dev(1, core), x_dev(-1, core), x_dev(0, 1 - core)):
        pl.semaphore_signal(barrier, inc=1, device_id={"tensor": t}, device_id_type=MESH)

    slot_rows = lax.broadcasted_iota(jnp.int32, (LANES, TOK), 0)
    sel_rt[...] = (slot_rows == ss_row[...]).astype(BF)
    send_g[...] = nn(sel_rt[...], g_ref[...]).astype(BF)
    pl.semaphore_wait(barrier, NDP - 1 + 3)

    def rows_of(d):
        return pl.ds(pl.multiple_of(d * CAP, CAP), CAP)

    def exchange(src, dst, s_sem, r_sem):
        def one(k, _):
            d = peer(k)
            pltpu.make_async_remote_copy(
                src_ref=src.at[rows_of(d)], dst_ref=dst.at[rows_of(me)],
                send_sem=s_sem, recv_sem=r_sem, device_id={"dp": d}, device_id_type=MESH,
            ).start()
            return 0

        lax.fori_loop(1, NDP, one, 0)
        dst[rows_of(me)] = src[rows_of(me)]

    def drain(ref, sem):
        whole = ref.at[pl.ds(0, LANES - CAP)]
        pltpu.make_async_copy(whole, whole, sem).wait()

    exchange(send_g, recv_g, sem_gs, sem_gr)
    kv_in = jnp.concatenate([k_ref[...], v_ref[...]], axis=1)
    send_x[NB] = nn(sel_rt[...], kv_in).astype(BF)
    exchange(send_x.at[NB], recv_x.at[NB], sem_xs.at[NB], sem_xr.at[NB])

    def push_q(j, _):
        cols = pl.ds(pl.multiple_of(j * BLK, BLK), BLK)
        send_x[j] = nn(sel_rt[...], q_ref[:, cols]).astype(BF)
        exchange(send_x.at[j], recv_x.at[j], sem_xs.at[j], sem_xr.at[j])
        return 0

    lax.fori_loop(0, NB, push_q, 0)

    slot_cols = lax.broadcasted_iota(jnp.int32, (TOK, LANES), 1)
    sel_r[...] = (slot_cols == ri_col[...]).astype(BF)
    sel_rt[...] = (slot_rows == ri_row[...]).astype(BF)
    key_at = lax.broadcasted_iota(jnp.int32, (TOK, TOK), 0)
    query_at = lax.broadcasted_iota(jnp.int32, (TOK, TOK), 1)
    seen = (doc_col[...] == doc_row[...]) & (key_at <= query_at)
    bias[...] = jnp.where(seen, 0.0, -1e30).astype(F32)
    dkv[...] = jnp.zeros_like(dkv)

    drain(recv_g, sem_gr)

    def feats(t, lo=0, n=PART):
        return pl.ds(pl.multiple_of(t * PART + lo, 16), n)

    mine = nn(sel_r[...], recv_g[...]).T.astype(BF)
    gt[feats(tp)] = mine

    def ring(idx, t, lo, n, dev):
        c = pltpu.make_async_remote_copy(
            src_ref=gt.at[feats(t, lo, n)], dst_ref=gt.at[feats(t, lo, n)],
            send_sem=sem_as.at[idx], recv_sem=sem_ar.at[idx],
            device_id={"tensor": dev}, device_id_type=MESH,
        )
        c.start()
        return c

    right, left, twin = x_dev(1, core), x_dev(-1, core), x_dev(0, 1 - core)
    far = x_dev(2, core)
    half = PART // 2
    cps = [
        ring(0, tp, 0, PART, right),
        ring(1, tp, 0, PART, left),
        ring(2, tp, 0, PART, twin),
    ]

    def arrived(idx, t, lo, n):
        ref = gt.at[feats(t, lo, n)]
        pltpu.make_async_copy(ref, ref, sem_ar.at[idx]).wait()

    arrived(0, left, 0, PART)
    cps.append(ring(3, left, 0, half, right))
    cps.append(ring(4, left, 0, PART, twin))
    arrived(1, right, 0, PART)
    cps.append(ring(5, right, half, half, left))
    cps.append(ring(6, right, 0, PART, twin))
    arrived(3, far, 0, half)
    arrived(5, far, half, half)
    cps.append(ring(7, far, 0, PART, twin))

    drain(recv_x.at[NB], sem_xr.at[NB])
    kv_f = nn(sel_r[...], recv_x[NB])
    kv[...] = kv_f.astype(BF)
    kvt[...] = kv_f.T.astype(BF)

    arrived(2, x_dev(0, 1 - core), 0, PART)
    arrived(4, x_dev(-1, 1 - core), 0, PART)
    arrived(6, x_dev(1, 1 - core), 0, PART)
    arrived(7, x_dev(2, 1 - core), 0, PART)

    inv = 1.0 / math.sqrt(HEAD_DIM)
    norm = 1.0 / math.sqrt(TOK * NDP)
    HALF = TOK // 2

    def head_block(j):
        rows = pl.ds(pl.multiple_of(j * BLK, BLK), BLK)
        hgt[...] = nn(w_ref[rows, :], gt[...]).astype(BF)
        qp = nn(sel_r[...], recv_x[j]).astype(BF)
        for h in range(2):
            hs = slice(h * HEAD_DIM, (h + 1) * HEAD_DIM)
            for b in range(2):
                kn = HALF * (b + 1)
                ps = slice(b * HALF, (b + 1) * HALF)
                qh = qp[ps, hs]
                keys, vals = kv[:kn, :HEAD_DIM], kv[:kn, HEAD_DIM:]
                s = nt(keys, qh) + bias[:kn, ps]
                top = jnp.max(s, axis=0, keepdims=True)
                e = jnp.exp((s - top) * inv)
                soft = e * (1.0 / jnp.sum(e, axis=0, keepdims=True))
                soft_half = soft.astype(BF)
                att[hs, ps] = nn(kvt[HEAD_DIM:, :kn], soft_half).astype(BF)
                hg = hgt[hs, ps]
                dp_ = nn(vals, hg)
                inner = jnp.sum(soft * dp_, axis=0, keepdims=True)
                ds = (soft * (dp_ - inner)).astype(BF)
                dqt[hs, ps] = (nn(kvt[:HEAD_DIM, :kn], ds) * inv).astype(BF)
                dkv[:kn, :HEAD_DIM] += nn(ds, qh)
                dkv[:kn, HEAD_DIM:] += nt(soft_half, hg)

        def weight_slab(y, _):
            rows = pl.ds(pl.multiple_of(y * SLAB, SLAB), SLAB)
            part[j, y] = (nt(gt[rows, :], att[...]) * norm).astype(BF).reshape(NZ, ROWS, BLK)
            return 0

        lax.fori_loop(0, NY, weight_slab, 0)

    def yid(k):
        return lax.rem(my_y + k + 2 * NY, NY)

    def zid(k):
        return lax.rem(my_z + k + 2 * NZ, NZ)

    def send(src, dst, ss, rs, dev):
        pltpu.make_async_remote_copy(
            src_ref=src, dst_ref=dst, send_sem=ss, recv_sem=rs,
            device_id={"dp": dev}, device_id_type=MESH,
        ).start()

    def landed(ref, sem):
        pltpu.make_async_copy(ref, ref, sem).wait()

    def sgn(j):
        return 1 - 2 * lax.rem(j, 2)

    def y_start(j):
        g = sgn(j)
        send(part.at[j, yid(2 * g)], ya.at[j], sem_ys.at[j, 0], sem_yr.at[j, 0], dp_dev(g, 0))
        send(part.at[j, yid(-g)], yb.at[j], sem_ys.at[j, 1], sem_yr.at[j, 1], dp_dev(-g, 0))

    def y_next(j):
        g = sgn(j)
        landed(ya.at[j], sem_yr.at[j, 0])
        ya[j] = (ya[j].astype(F32) + part[j, yid(g)].astype(F32)).astype(BF)
        send(ya.at[j], yc.at[j], sem_ys.at[j, 2], sem_yr.at[j, 2], dp_dev(g, 0))

    def y_end(j):
        g = sgn(j)
        landed(yb.at[j], sem_yr.at[j, 1])
        landed(yc.at[j], sem_yr.at[j, 2])
        yt[j] = (yb[j].astype(F32) + yc[j].astype(F32) + part[j, my_y].astype(F32)).astype(BF)
        send(yt.at[j, zid(4 * g)], za.at[j, 0], sem_zs.at[j, 0], sem_zr.at[j, 0], dp_dev(0, g))
        send(yt.at[j, zid(-3 * g)], zb.at[j, 0], sem_zs.at[j, 4], sem_zr.at[j, 4], dp_dev(0, -g))

    def z_next(j, s):
        g = sgn(j)
        landed(za.at[j, s], sem_zr.at[j, s])
        if s < 3:
            za[j, s] = (za[j, s].astype(F32) + yt[j, zid((3 - s) * g)].astype(F32)).astype(BF)
            send(za.at[j, s], za.at[j, s + 1], sem_zs.at[j, s + 1], sem_zr.at[j, s + 1], dp_dev(0, g))
        if s < 3:
            landed(zb.at[j, s], sem_zr.at[j, 4 + s])
        if s < 2:
            zb[j, s] = (zb[j, s].astype(F32) + yt[j, zid((s - 2) * g)].astype(F32)).astype(BF)
            send(zb.at[j, s], zb.at[j, s + 1], sem_zs.at[j, 5 + s], sem_zr.at[j, 5 + s], dp_dev(0, -g))
        if s == 3:
            cols = pl.ds(pl.multiple_of(j * BLK, BLK), BLK)
            wg_ref[:, cols] = za[j, 3].astype(F32) + zb[j, 2].astype(F32) + yt[j, my_z].astype(F32)

    def step(j, _):
        drain(recv_x.at[j], sem_xr.at[j])
        head_block(j)
        y_start(j)
        back[j] = nt(sel_rt[...], dqt[...]).astype(BF)
        exchange(back.at[j], home.at[j], sem_bs.at[j], sem_br.at[j])

        @pl.when(j >= 1)
        def _():
            y_next(j - 1)

        @pl.when(j >= 2)
        def _():
            y_end(j - 2)

        return 0

    lax.fori_loop(0, NB, step, 0)

    lane = lax.broadcasted_iota(jnp.int32, (TOK, 2 * HEAD_DIM), 1)
    dkv_h = (dkv[...] * jnp.where(lane < HEAD_DIM, inv, 1.0)).astype(BF)
    back[NB] = nn(sel_rt[...], dkv_h).astype(BF)
    exchange(back.at[NB], home.at[NB], sem_bs.at[NB], sem_br.at[NB])

    sel_r[...] = (slot_cols == ss_col[...]).astype(BF)
    y_next(NB - 1)
    for s in range(3):
        z_next(0, s)
    y_end(NB - 2)
    z_next(0, 3)
    for s in range(4):
        z_next(1, s)

    def settle(j):
        drain(home.at[j], sem_br.at[j])
        return nn(sel_r[...], home[j]).astype(BF)

    qg_ref[:, 0:BLK] = settle(0)
    y_end(NB - 1)
    z_next(2, 0)
    qg_ref[:, BLK:2 * BLK] = settle(1)
    z_next(2, 1)
    z_next(3, 0)
    z_next(2, 2)
    z_next(3, 1)
    z_next(2, 3)
    z_next(3, 2)
    z_next(3, 3)
    qg_ref[:, 2 * BLK:3 * BLK] = settle(2)
    qg_ref[:, 3 * BLK:] = settle(3)
    got = settle(NB)
    kg_ref[...] = got[:, :HEAD_DIM]
    vg_ref[...] = got[:, HEAD_DIM:]

    drain(send_g, sem_gs)

    def sent(j, _):
        drain(send_x.at[j], sem_xs.at[j])
        drain(back.at[j], sem_bs.at[j])
        return 0

    lax.fori_loop(0, NB + 1, sent, 0)
    for c in cps:
        c.wait_send()

    def ring_sent(j, _):
        landed(ya.at[j], sem_ys.at[j, 0])
        landed(ya.at[j], sem_ys.at[j, 1])
        landed(ya.at[j], sem_ys.at[j, 2])
        for s in range(7):
            landed(za.at[j, 0], sem_zs.at[j, s])
        return 0

    lax.fori_loop(0, NB, ring_sent, 0)


def shards(queries, keys, values, out_grad, out_weight, send_slot, recv_index, packed_doc):
    row = lambda a: a.reshape(1, TOK)
    col = lambda a: a.reshape(TOK, 1)
    vmem = pl.BlockSpec(memory_space=pltpu.VMEM)
    dma = pltpu.SemaphoreType.DMA
    return pl.pallas_call(
        kernel,
        out_shape=(
            jax.ShapeDtypeStruct((TOK, NB * BLK), BF),
            jax.ShapeDtypeStruct((TOK, HEAD_DIM), BF),
            jax.ShapeDtypeStruct((TOK, HEAD_DIM), BF),
            jax.ShapeDtypeStruct((ROWS, NB * BLK), F32),
        ),
        in_specs=[vmem] * 11,
        out_specs=(vmem,) * 4,
        scratch_shapes=[
            pltpu.VMEM((LANES, PART), BF),
            pltpu.VMEM((LANES, PART), BF),
            pltpu.VMEM((NB + 1, LANES, BLK), BF),
            pltpu.VMEM((NB + 1, LANES, BLK), BF),
            pltpu.VMEM((NB + 1, LANES, BLK), BF),
            pltpu.VMEM((NB + 1, LANES, BLK), BF),
            pltpu.VMEM((TOK, LANES), BF),
            pltpu.VMEM((LANES, TOK), BF),
            pltpu.VMEM((FEAT, TOK), BF),
            pltpu.VMEM((TOK, TOK), F32),
            pltpu.VMEM((TOK, BLK), BF),
            pltpu.VMEM((BLK, TOK), BF),
            pltpu.VMEM((TOK, BLK), F32),
            pltpu.VMEM((BLK, TOK), BF),
            pltpu.VMEM((BLK, TOK), BF),
            pltpu.VMEM((BLK, TOK), BF),
            pltpu.VMEM((NB, NY, NZ, ROWS, BLK), BF),
            pltpu.VMEM((NB, NZ, ROWS, BLK), BF),
            pltpu.VMEM((NB, NZ, ROWS, BLK), BF),
            pltpu.VMEM((NB, NZ, ROWS, BLK), BF),
            pltpu.VMEM((NB, NZ, ROWS, BLK), BF),
            pltpu.VMEM((NB, 4, ROWS, BLK), BF),
            pltpu.VMEM((NB, 3, ROWS, BLK), BF),
            dma, dma,
            dma((NB + 1,)), dma((NB + 1,)),
            dma((NB + 1,)), dma((NB + 1,)),
            dma((8,)), dma((8,)),
            dma((NB, 3)), dma((NB, 3)),
            dma((NB, 7)), dma((NB, 7)),
        ],
        compiler_params=pltpu.CompilerParams(
            collective_id=1, has_side_effects=True, vmem_limit_bytes=60 << 20
        ),
        name="packed_attention_backward",
    )(
        queries, keys, values, out_grad, out_weight,
        row(send_slot), col(send_slot), row(recv_index), col(recv_index),
        row(packed_doc), col(packed_doc),
    )


def solution(mesh):
    both = P("dp", "tensor")
    return jax.shard_map(
        shards,
        mesh=mesh,
        in_specs=(both, both, both, both, P("tensor", None), P("dp"), P("dp"), P("dp")),
        out_specs=(both, both, both, both),
        check_vma=False,
    )
```

```python
import functools
import math

import jax
import jax.numpy as jnp
from jax import lax
from jax.experimental import pallas as pl
from jax.experimental.pallas import tpu as pltpu
from jax.sharding import PartitionSpec as P

MESH = pl.DeviceIdType.MESH
BF = jnp.bfloat16
F32 = jnp.float32
CAP = 32
HEAD_DIM = 128
NY = 4
NZ = 8
NX = 4
NDP = NY * NZ
TOK = 512
LANES = NDP * CAP
BLK = 256
NB = 4
PART = 384
FEAT = 3072
ROWS = FEAT // NDP
SLAB = NZ * ROWS


def nn(a, b):
    return lax.dot_general(a, b, (((1,), (0,)), ((), ())), preferred_element_type=F32)


def nt(a, b):
    return lax.dot_general(a, b, (((1,), (1,)), ((), ())), preferred_element_type=F32)


def column(row_ref):
    return jnp.broadcast_to(row_ref[...], (HEAD_DIM, TOK)).T[:, :1]


def kernel(
    q_hbm, k_hbm, v_hbm, g_ref, w_hbm, ss_row, ri_row, doc_row,
    qg_ref, kg_ref, vg_ref, wg_ref,
    q_ref, k_ref, v_ref, w_ref, sem_in,
    send_g, recv_g, send_x, recv_x, back, home,
    sel_r, sel_rt, gt, bias, kv, kvt, dkv, hgt, att, dqt,
    part, ya, yb, yc, yt, za, zb,
    sem_gs, sem_gr, sem_xs, sem_xr, sem_bs, sem_br, sem_as, sem_ar, sem_ys, sem_yr, sem_zs, sem_zr,
):
    me = lax.axis_index("dp")
    tp = lax.axis_index("tensor")
    my_y, my_z = me // NZ, lax.rem(me, NZ)
    my_x, core = tp // 2, lax.rem(tp, 2)

    def peer(k):
        return lax.rem(my_y + k // NZ, NY) * NZ + lax.rem(my_z + 3 * k, NZ)

    def x_dev(dx, c):
        return lax.rem(my_x + dx + NX, NX) * 2 + c

    def dp_dev(dy, dz):
        return lax.rem(my_y + dy + NY, NY) * NZ + lax.rem(my_z + dz + NZ, NZ)

    loads = [
        pltpu.make_async_copy(src, dst, sem_in.at[i])
        for i, (src, dst) in enumerate(
            ((k_hbm, k_ref), (v_hbm, v_ref), (q_hbm, q_ref), (w_hbm, w_ref))
        )
    ]
    for c in loads:
        c.start()

    barrier = pltpu.get_barrier_semaphore()

    def greet(k, _):
        pl.semaphore_signal(barrier, inc=1, device_id={"dp": peer(k)}, device_id_type=MESH)
        return 0

    lax.fori_loop(1, NDP, greet, 0)
    for t in (x_dev(1, core), x_dev(-1, core), x_dev(0, 1 - core)):
        pl.semaphore_signal(barrier, inc=1, device_id={"tensor": t}, device_id_type=MESH)

    slot_rows = lax.broadcasted_iota(jnp.int32, (LANES, TOK), 0)
    sel_rt[...] = (slot_rows == ss_row[...]).astype(BF)
    send_g[...] = nn(sel_rt[...], g_ref[...]).astype(BF)
    pl.semaphore_wait(barrier, NDP - 1 + 3)

    def rows_of(d):
        return pl.ds(pl.multiple_of(d * CAP, CAP), CAP)

    def exchange(src, dst, s_sem, r_sem):
        def one(k, _):
            d = peer(k)
            pltpu.make_async_remote_copy(
                src_ref=src.at[rows_of(d)], dst_ref=dst.at[rows_of(me)],
                send_sem=s_sem, recv_sem=r_sem, device_id={"dp": d}, device_id_type=MESH,
            ).start()
            return 0

        lax.fori_loop(1, NDP, one, 0)
        dst[rows_of(me)] = src[rows_of(me)]

    def drain(ref, sem):
        whole = ref.at[pl.ds(0, LANES - CAP)]
        pltpu.make_async_copy(whole, whole, sem).wait()

    exchange(send_g, recv_g, sem_gs, sem_gr)
    loads[0].wait()
    loads[1].wait()
    kv_in = jnp.concatenate([k_ref[...], v_ref[...]], axis=1)
    send_x[NB] = nn(sel_rt[...], kv_in).astype(BF)
    exchange(send_x.at[NB], recv_x.at[NB], sem_xs.at[NB], sem_xr.at[NB])

    def push_q(j, _):
        cols = pl.ds(pl.multiple_of(j * BLK, BLK), BLK)
        send_x[j] = nn(sel_rt[...], q_ref[:, cols]).astype(BF)
        exchange(send_x.at[j], recv_x.at[j], sem_xs.at[j], sem_xr.at[j])
        return 0

    loads[2].wait()
    lax.fori_loop(0, NB, push_q, 0)

    slot_cols = lax.broadcasted_iota(jnp.int32, (TOK, LANES), 1)
    sel_r[...] = (slot_cols == column(ri_row)).astype(BF)
    sel_rt[...] = (slot_rows == ri_row[...]).astype(BF)
    key_at = lax.broadcasted_iota(jnp.int32, (TOK, TOK), 0)
    query_at = lax.broadcasted_iota(jnp.int32, (TOK, TOK), 1)
    seen = (column(doc_row) == doc_row[...]) & (key_at <= query_at)
    bias[...] = jnp.where(seen, 0.0, -1e30).astype(F32)
    dkv[...] = jnp.zeros_like(dkv)

    drain(recv_g, sem_gr)

    def feats(t, lo=0, n=PART):
        return pl.ds(pl.multiple_of(t * PART + lo, 16), n)

    mine = nn(sel_r[...], recv_g[...]).T.astype(BF)
    gt[feats(tp)] = mine

    def ring(idx, t, lo, n, dev):
        c = pltpu.make_async_remote_copy(
            src_ref=gt.at[feats(t, lo, n)], dst_ref=gt.at[feats(t, lo, n)],
            send_sem=sem_as.at[idx], recv_sem=sem_ar.at[idx],
            device_id={"tensor": dev}, device_id_type=MESH,
        )
        c.start()
        return c

    right, left, twin = x_dev(1, core), x_dev(-1, core), x_dev(0, 1 - core)
    far = x_dev(2, core)
    half = PART // 2
    cps = [
        ring(0, tp, 0, PART, right),
        ring(1, tp, 0, PART, left),
        ring(2, tp, 0, PART, twin),
    ]

    def arrived(idx, t, lo, n):
        ref = gt.at[feats(t, lo, n)]
        pltpu.make_async_copy(ref, ref, sem_ar.at[idx]).wait()

    arrived(0, left, 0, PART)
    cps.append(ring(3, left, 0, half, right))
    cps.append(ring(4, left, 0, PART, twin))
    arrived(1, right, 0, PART)
    cps.append(ring(5, right, half, half, left))
    cps.append(ring(6, right, 0, PART, twin))
    arrived(3, far, 0, half)
    arrived(5, far, half, half)
    cps.append(ring(7, far, 0, PART, twin))

    drain(recv_x.at[NB], sem_xr.at[NB])
    kv_f = nn(sel_r[...], recv_x[NB])
    kv[...] = kv_f.astype(BF)
    kvt[...] = kv_f.T.astype(BF)

    arrived(2, x_dev(0, 1 - core), 0, PART)
    arrived(4, x_dev(-1, 1 - core), 0, PART)
    arrived(6, x_dev(1, 1 - core), 0, PART)
    arrived(7, x_dev(2, 1 - core), 0, PART)

    loads[3].wait()
    inv = 1.0 / math.sqrt(HEAD_DIM)
    norm = 1.0 / math.sqrt(TOK * NDP)
    HALF = TOK // 2

    def head_block(j):
        rows = pl.ds(pl.multiple_of(j * BLK, BLK), BLK)
        hgt[...] = nn(w_ref[rows, :], gt[...]).astype(BF)
        qp = nn(sel_r[...], recv_x[j]).astype(BF)
        for h in range(2):
            hs = slice(h * HEAD_DIM, (h + 1) * HEAD_DIM)
            for b in range(2):
                kn = HALF * (b + 1)
                ps = slice(b * HALF, (b + 1) * HALF)
                qh = qp[ps, hs]
                keys, vals = kv[:kn, :HEAD_DIM], kv[:kn, HEAD_DIM:]
                s = nt(keys, qh) + bias[:kn, ps]
                top = jnp.max(s, axis=0, keepdims=True)
                e = jnp.exp((s - top) * inv)
                soft = e * (1.0 / jnp.sum(e, axis=0, keepdims=True))
                soft_half = soft.astype(BF)
                att[hs, ps] = nn(kvt[HEAD_DIM:, :kn], soft_half).astype(BF)
                hg = hgt[hs, ps]
                dp_ = nn(vals, hg)
                inner = jnp.sum(soft * dp_, axis=0, keepdims=True)
                ds = (soft * (dp_ - inner)).astype(BF)
                dqt[hs, ps] = (nn(kvt[:HEAD_DIM, :kn], ds) * inv).astype(BF)
                dkv[:kn, :HEAD_DIM] += nn(ds, qh)
                dkv[:kn, HEAD_DIM:] += nt(soft_half, hg)

        def weight_slab(y, _):
            rows = pl.ds(pl.multiple_of(y * SLAB, SLAB), SLAB)
            part[j, y] = (nt(gt[rows, :], att[...]) * norm).astype(BF).reshape(NZ, ROWS, BLK)
            return 0

        lax.fori_loop(0, NY, weight_slab, 0)

    def yid(k):
        return lax.rem(my_y + k + 2 * NY, NY)

    def zid(k):
        return lax.rem(my_z + k + 2 * NZ, NZ)

    def send(src, dst, ss, rs, dev):
        pltpu.make_async_remote_copy(
            src_ref=src, dst_ref=dst, send_sem=ss, recv_sem=rs,
            device_id={"dp": dev}, device_id_type=MESH,
        ).start()

    def landed(ref, sem):
        pltpu.make_async_copy(ref, ref, sem).wait()

    def sgn(j):
        return 1 - 2 * lax.rem(j, 2)

    def y_start(j):
        g = sgn(j)
        send(part.at[j, yid(2 * g)], ya.at[j], sem_ys.at[j, 0], sem_yr.at[j, 0], dp_dev(g, 0))
        send(part.at[j, yid(-g)], yb.at[j], sem_ys.at[j, 1], sem_yr.at[j, 1], dp_dev(-g, 0))

    def y_next(j):
        g = sgn(j)
        landed(ya.at[j], sem_yr.at[j, 0])
        ya[j] = (ya[j].astype(F32) + part[j, yid(g)].astype(F32)).astype(BF)
        send(ya.at[j], yc.at[j], sem_ys.at[j, 2], sem_yr.at[j, 2], dp_dev(g, 0))

    def y_end(j):
        g = sgn(j)
        landed(yb.at[j], sem_yr.at[j, 1])
        landed(yc.at[j], sem_yr.at[j, 2])
        yt[j] = (yb[j].astype(F32) + yc[j].astype(F32) + part[j, my_y].astype(F32)).astype(BF)
        send(yt.at[j, zid(4 * g)], za.at[j, 0], sem_zs.at[j, 0], sem_zr.at[j, 0], dp_dev(0, g))
        send(yt.at[j, zid(-3 * g)], zb.at[j, 0], sem_zs.at[j, 4], sem_zr.at[j, 4], dp_dev(0, -g))

    def z_next(j, s):
        g = sgn(j)
        landed(za.at[j, s], sem_zr.at[j, s])
        if s < 3:
            za[j, s] = (za[j, s].astype(F32) + yt[j, zid((3 - s) * g)].astype(F32)).astype(BF)
            send(za.at[j, s], za.at[j, s + 1], sem_zs.at[j, s + 1], sem_zr.at[j, s + 1], dp_dev(0, g))
        if s < 3:
            landed(zb.at[j, s], sem_zr.at[j, 4 + s])
        if s < 2:
            zb[j, s] = (zb[j, s].astype(F32) + yt[j, zid((s - 2) * g)].astype(F32)).astype(BF)
            send(zb.at[j, s], zb.at[j, s + 1], sem_zs.at[j, 5 + s], sem_zr.at[j, 5 + s], dp_dev(0, -g))
        if s == 3:
            cols = pl.ds(pl.multiple_of(j * BLK, BLK), BLK)
            wg_ref[:, cols] = za[j, 3].astype(F32) + zb[j, 2].astype(F32) + yt[j, my_z].astype(F32)

    def step(j, _):
        drain(recv_x.at[j], sem_xr.at[j])
        head_block(j)
        y_start(j)
        back[j] = nt(sel_rt[...], dqt[...]).astype(BF)
        exchange(back.at[j], home.at[j], sem_bs.at[j], sem_br.at[j])

        @pl.when(j >= 1)
        def _():
            y_next(j - 1)

        return 0

    lax.fori_loop(0, NB, step, 0)

    lane = lax.broadcasted_iota(jnp.int32, (TOK, 2 * HEAD_DIM), 1)
    dkv_h = (dkv[...] * jnp.where(lane < HEAD_DIM, inv, 1.0)).astype(BF)
    back[NB] = nn(sel_rt[...], dkv_h).astype(BF)
    exchange(back.at[NB], home.at[NB], sem_bs.at[NB], sem_br.at[NB])

    sel_r[...] = (slot_cols == column(ss_row)).astype(BF)
    def settle(j):
        drain(home.at[j], sem_br.at[j])
        return nn(sel_r[...], home[j]).astype(BF)

    y_end(0)
    y_end(1)
    z_next(0, 0)
    y_next(3)
    y_end(2)
    z_next(1, 0)
    z_next(0, 1)
    z_next(1, 1)
    z_next(2, 0)
    z_next(0, 2)
    y_end(3)
    z_next(1, 2)
    z_next(2, 1)
    z_next(0, 3)
    z_next(3, 0)
    z_next(1, 3)
    z_next(2, 2)
    z_next(3, 1)
    z_next(2, 3)
    z_next(3, 2)
    z_next(3, 3)
    for j in range(NB):
        qg_ref[:, j * BLK:(j + 1) * BLK] = settle(j)
    got = settle(NB)
    kg_ref[...] = got[:, :HEAD_DIM]
    vg_ref[...] = got[:, HEAD_DIM:]

    drain(send_g, sem_gs)

    def sent(j, _):
        drain(send_x.at[j], sem_xs.at[j])
        drain(back.at[j], sem_bs.at[j])
        return 0

    lax.fori_loop(0, NB + 1, sent, 0)
    for c in cps:
        c.wait_send()

    def ring_sent(j, _):
        landed(ya.at[j], sem_ys.at[j, 0])
        landed(ya.at[j], sem_ys.at[j, 1])
        landed(ya.at[j], sem_ys.at[j, 2])
        for s in range(7):
            landed(za.at[j, 0], sem_zs.at[j, s])
        return 0

    lax.fori_loop(0, NB, ring_sent, 0)


def hand_on(*refs):
    for src, dst in zip(refs[:4], refs[4:]):
        dst[...] = src[...]


def shards(queries, keys, values, out_grad, out_weight, send_slot, recv_index, packed_doc):
    row = lambda a: a.reshape(1, TOK)
    vmem = pl.BlockSpec(memory_space=pltpu.VMEM)
    hbm = pl.BlockSpec(memory_space=pl.ANY)
    dma = pltpu.SemaphoreType.DMA
    grads = pl.pallas_call(
        kernel,
        out_shape=(
            jax.ShapeDtypeStruct((TOK, NB * BLK), BF),
            jax.ShapeDtypeStruct((TOK, HEAD_DIM), BF),
            jax.ShapeDtypeStruct((TOK, HEAD_DIM), BF),
            jax.ShapeDtypeStruct((ROWS, NB * BLK), F32),
        ),
        in_specs=[hbm, hbm, hbm, vmem, hbm, vmem, vmem, vmem],
        out_specs=(vmem,) * 4,
        scratch_shapes=[
            pltpu.VMEM((TOK, NB * BLK), BF),
            pltpu.VMEM((TOK, HEAD_DIM), BF),
            pltpu.VMEM((TOK, HEAD_DIM), BF),
            pltpu.VMEM((NB * BLK, FEAT), BF),
            dma((4,)),
            pltpu.VMEM((LANES, PART), BF),
            pltpu.VMEM((LANES, PART), BF),
            pltpu.VMEM((NB + 1, LANES, BLK), BF),
            pltpu.VMEM((NB + 1, LANES, BLK), BF),
            pltpu.VMEM((NB + 1, LANES, BLK), BF),
            pltpu.VMEM((NB + 1, LANES, BLK), BF),
            pltpu.VMEM((TOK, LANES), BF),
            pltpu.VMEM((LANES, TOK), BF),
            pltpu.VMEM((FEAT, TOK), BF),
            pltpu.VMEM((TOK, TOK), F32),
            pltpu.VMEM((TOK, BLK), BF),
            pltpu.VMEM((BLK, TOK), BF),
            pltpu.VMEM((TOK, BLK), F32),
            pltpu.VMEM((BLK, TOK), BF),
            pltpu.VMEM((BLK, TOK), BF),
            pltpu.VMEM((BLK, TOK), BF),
            pltpu.VMEM((NB, NY, NZ, ROWS, BLK), BF),
            pltpu.VMEM((NB, NZ, ROWS, BLK), BF),
            pltpu.VMEM((NB, NZ, ROWS, BLK), BF),
            pltpu.VMEM((NB, NZ, ROWS, BLK), BF),
            pltpu.VMEM((NB, NZ, ROWS, BLK), BF),
            pltpu.VMEM((NB, 4, ROWS, BLK), BF),
            pltpu.VMEM((NB, 3, ROWS, BLK), BF),
            dma, dma,
            dma((NB + 1,)), dma((NB + 1,)),
            dma((NB + 1,)), dma((NB + 1,)),
            dma((8,)), dma((8,)),
            dma((NB, 3)), dma((NB, 3)),
            dma((NB, 7)), dma((NB, 7)),
        ],
        compiler_params=pltpu.CompilerParams(
            collective_id=1, has_side_effects=True, vmem_limit_bytes=60 << 20
        ),
        name="packed_attention_backward",
    )(
        queries, keys, values, out_grad, out_weight,
        row(send_slot), row(recv_index), row(packed_doc),
    )
    return pl.pallas_call(
        hand_on,
        out_shape=tuple(jax.ShapeDtypeStruct(a.shape, a.dtype) for a in grads),
        in_specs=[vmem] * 4,
        out_specs=(vmem,) * 4,
        name="results",
    )(*grads)


def solution(mesh):
    both = P("dp", "tensor")
    return jax.shard_map(
        shards,
        mesh=mesh,
        in_specs=(both, both, both, both, P("tensor", None), P("dp"), P("dp"), P("dp")),
        out_specs=(both, both, both, both),
        check_vma=False,
    )
```

```python
import functools
import math

import jax
import jax.numpy as jnp
from jax import lax
from jax.experimental import pallas as pl
from jax.experimental.pallas import tpu as pltpu
from jax.sharding import PartitionSpec as P

MESH = pl.DeviceIdType.MESH
BF = jnp.bfloat16
F32 = jnp.float32
CAP = 32
HEAD_DIM = 128
NY = 4
NZ = 8
NX = 4
NDP = NY * NZ
TOK = 512
LANES = NDP * CAP
BLK = 256
NB = 4
PART = 384
FEAT = 3072
ROWS = FEAT // NDP
SLAB = NZ * ROWS
HALF = TOK // 2


def nn(a, b):
    return lax.dot_general(a, b, (((1,), (0,)), ((), ())), preferred_element_type=F32)


def nt(a, b):
    return lax.dot_general(a, b, (((1,), (1,)), ((), ())), preferred_element_type=F32)


def column(row_ref):
    return jnp.broadcast_to(row_ref[...], (HEAD_DIM, TOK)).T[:, :1]


def kernel(
    q_hbm, k_hbm, v_hbm, g_ref, w_hbm, ss_row, ri_row, doc_row,
    qg_ref, kg_ref, vg_ref, wg_ref,
    q_ref, k_ref, v_ref, w_ref, sem_in,
    send_g, recv_g, send_x, recv_x, back, home,
    sel_r, sel_rt, gt, bias, kv, kvt, dkv, hgt, dqt,
    weights, g4, att4, yt, za, zb,
    sem_gs, sem_gr, sem_xs, sem_xr, sem_bs, sem_br, sem_as, sem_ar, sem_ys, sem_yr, sem_zs, sem_zr,
    sem_4s, sem_4r,
):
    me = lax.axis_index("dp")
    tp = lax.axis_index("tensor")
    my_y, my_z = me // NZ, lax.rem(me, NZ)
    my_x, core = tp // 2, lax.rem(tp, 2)

    def peer(k):
        return lax.rem(my_y + k // NZ, NY) * NZ + lax.rem(my_z + 3 * k, NZ)

    def x_dev(dx, c):
        return lax.rem(my_x + dx + NX, NX) * 2 + c

    def dp_dev(dy, dz):
        return lax.rem(my_y + dy + NY, NY) * NZ + lax.rem(my_z + dz + NZ, NZ)

    loads = [
        pltpu.make_async_copy(src, dst, sem_in.at[i])
        for i, (src, dst) in enumerate(
            ((k_hbm, k_ref), (v_hbm, v_ref), (q_hbm, q_ref), (w_hbm, w_ref))
        )
    ]
    for c in loads:
        c.start()

    barrier = pltpu.get_barrier_semaphore()

    def greet(k, _):
        pl.semaphore_signal(barrier, inc=1, device_id={"dp": peer(k)}, device_id_type=MESH)
        return 0

    lax.fori_loop(1, NDP, greet, 0)
    for t in (x_dev(1, core), x_dev(-1, core), x_dev(0, 1 - core)):
        pl.semaphore_signal(barrier, inc=1, device_id={"tensor": t}, device_id_type=MESH)

    slot_rows = lax.broadcasted_iota(jnp.int32, (LANES, TOK), 0)
    sel_rt[...] = (slot_rows == ss_row[...]).astype(BF)
    send_g[...] = nn(sel_rt[...], g_ref[...]).astype(BF)
    pl.semaphore_wait(barrier, NDP - 1 + 3)

    def rows_of(d):
        return pl.ds(pl.multiple_of(d * CAP, CAP), CAP)

    def exchange(src, dst, s_sem, r_sem, lo=1, hi=NDP):
        def one(k, _):
            d = peer(k)
            pltpu.make_async_remote_copy(
                src_ref=src.at[rows_of(d)], dst_ref=dst.at[rows_of(me)],
                send_sem=s_sem, recv_sem=r_sem, device_id={"dp": d}, device_id_type=MESH,
            ).start()
            return 0

        lax.fori_loop(lo, hi, one, 0)
        if lo == 1:
            dst[rows_of(me)] = src[rows_of(me)]

    def drain(ref, sem):
        whole = ref.at[pl.ds(0, LANES - CAP)]
        pltpu.make_async_copy(whole, whole, sem).wait()

    exchange(send_g, recv_g, sem_gs, sem_gr)
    loads[0].wait()
    loads[1].wait()
    kv_in = jnp.concatenate([k_ref[...], v_ref[...]], axis=1)
    send_x[NB] = nn(sel_rt[...], kv_in).astype(BF)
    exchange(send_x.at[NB], recv_x.at[NB], sem_xs.at[NB], sem_xr.at[NB])

    def push_q(j, _):
        cols = pl.ds(pl.multiple_of(j * BLK, BLK), BLK)
        send_x[j] = nn(sel_rt[...], q_ref[:, cols]).astype(BF)
        exchange(send_x.at[j], recv_x.at[j], sem_xs.at[j], sem_xr.at[j])
        return 0

    loads[2].wait()
    lax.fori_loop(0, NB, push_q, 0)

    slot_cols = lax.broadcasted_iota(jnp.int32, (TOK, LANES), 1)
    sel_r[...] = (slot_cols == column(ri_row)).astype(BF)
    sel_rt[...] = (slot_rows == ri_row[...]).astype(BF)
    key_at = lax.broadcasted_iota(jnp.int32, (TOK, TOK), 0)
    query_at = lax.broadcasted_iota(jnp.int32, (TOK, TOK), 1)
    seen = (column(doc_row) == doc_row[...]) & (key_at <= query_at)
    bias[...] = jnp.where(seen, 0.0, -1e30).astype(F32)
    dkv[...] = jnp.zeros_like(dkv)

    drain(recv_g, sem_gr)

    def feats(t, lo=0, n=PART):
        return pl.ds(pl.multiple_of(t * PART + lo, 16), n)

    mine = nn(sel_r[...], recv_g[...]).T.astype(BF)
    gt[feats(tp)] = mine

    def ring(idx, t, lo, n, dev):
        c = pltpu.make_async_remote_copy(
            src_ref=gt.at[feats(t, lo, n)], dst_ref=gt.at[feats(t, lo, n)],
            send_sem=sem_as.at[idx], recv_sem=sem_ar.at[idx],
            device_id={"tensor": dev}, device_id_type=MESH,
        )
        c.start()
        return c

    right, left, twin = x_dev(1, core), x_dev(-1, core), x_dev(0, 1 - core)
    far = x_dev(2, core)
    half = PART // 2
    cps = [
        ring(0, tp, 0, PART, right),
        ring(1, tp, 0, PART, left),
        ring(2, tp, 0, PART, twin),
    ]

    def arrived(idx, t, lo, n):
        ref = gt.at[feats(t, lo, n)]
        pltpu.make_async_copy(ref, ref, sem_ar.at[idx]).wait()

    arrived(0, left, 0, PART)
    cps.append(ring(3, left, 0, half, right))
    cps.append(ring(4, left, 0, PART, twin))
    arrived(1, right, 0, PART)
    cps.append(ring(5, right, half, half, left))
    cps.append(ring(6, right, 0, PART, twin))
    arrived(3, far, 0, half)
    arrived(5, far, half, half)
    cps.append(ring(7, far, 0, PART, twin))

    drain(recv_x.at[NB], sem_xr.at[NB])
    kv_f = nn(sel_r[...], recv_x[NB])
    kv[...] = kv_f.astype(BF)
    kvt[...] = kv_f.T.astype(BF)

    arrived(2, x_dev(0, 1 - core), 0, PART)
    arrived(4, x_dev(-1, 1 - core), 0, PART)
    arrived(6, x_dev(1, 1 - core), 0, PART)
    arrived(7, x_dev(2, 1 - core), 0, PART)

    loads[3].wait()
    inv = 1.0 / math.sqrt(HEAD_DIM)
    norm = 1.0 / math.sqrt(TOK * NDP)

    def head_block(j):
        rows = pl.ds(pl.multiple_of(j * BLK, BLK), BLK)
        qp = nn(sel_r[...], recv_x[j]).astype(BF)
        places = [(h, b) for h in range(2) for b in range(2)]

        def cut(h, b):
            kn = HALF * (b + 1)
            return kn, slice(h * HEAD_DIM, (h + 1) * HEAD_DIM), slice(b * HALF, (b + 1) * HALF)

        for h, b in places:
            kn, hs, ps = cut(h, b)
            s = nt(kv[:kn, :HEAD_DIM], qp[ps, hs]) + bias[:kn, ps]
            top = jnp.max(s, axis=0, keepdims=True)
            e = jnp.exp((s - top) * inv)
            soft = e * (1.0 / jnp.sum(e, axis=0, keepdims=True))
            weights[h, b, :kn] = soft
            att4[j, my_y, hs, ps] = nn(kvt[HEAD_DIM:, :kn], soft.astype(BF)).astype(BF)

        a_start(j)
        hgt[...] = nn(w_ref[rows, :], gt[...]).astype(BF)
        for h, b in places:
            kn, hs, ps = cut(h, b)
            soft = weights[h, b, :kn]
            hg = hgt[hs, ps]
            dp_ = nn(kv[:kn, HEAD_DIM:], hg)
            inner = jnp.sum(soft * dp_, axis=0, keepdims=True)
            ds = (soft * (dp_ - inner)).astype(BF)
            dqt[hs, ps] = (nn(kvt[:HEAD_DIM, :kn], ds) * inv).astype(BF)
            dkv[:kn, :HEAD_DIM] += nn(ds, qp[ps, hs])
            dkv[:kn, HEAD_DIM:] += nt(soft.astype(BF), hg)

    def yid(k):
        return lax.rem(my_y + k + 2 * NY, NY)

    def zid(k):
        return lax.rem(my_z + k + 2 * NZ, NZ)

    def send(src, dst, ss, rs, dev):
        pltpu.make_async_remote_copy(
            src_ref=src, dst_ref=dst, send_sem=ss, recv_sem=rs,
            device_id={"dp": dev}, device_id_type=MESH,
        ).start()

    def landed(ref, sem):
        pltpu.make_async_copy(ref, ref, sem).wait()

    def sgn(j):
        return 1 - 2 * lax.rem(j, 2)

    def a_start(j):
        mine_ = att4.at[j, my_y]
        send(mine_, mine_, sem_ys.at[j, 0], sem_yr.at[j, 0], dp_dev(1, 0))
        send(mine_, mine_, sem_ys.at[j, 1], sem_yr.at[j, 1], dp_dev(-1, 0))

    low, high = pl.ds(0, BLK // 2), pl.ds(BLK // 2, BLK // 2)

    def a_next(j):
        below, above = att4.at[j, yid(-1)], att4.at[j, yid(1)]
        landed(below, sem_yr.at[j, 0])
        send(below.at[low], below.at[low], sem_ys.at[j, 2], sem_yr.at[j, 2], dp_dev(1, 0))
        landed(above, sem_yr.at[j, 1])
        send(above.at[high], above.at[high], sem_ys.at[j, 3], sem_yr.at[j, 3], dp_dev(-1, 0))

    def a_end(j):
        g = sgn(j)
        opposite = att4.at[j, yid(2)]
        landed(opposite.at[low], sem_yr.at[j, 2])
        landed(opposite.at[high], sem_yr.at[j, 3])

        def slab(i, _):
            rows = pl.ds(pl.multiple_of(i * 2 * ROWS, 2 * ROWS), 2 * ROWS)
            tot = nt(g4[0, rows, :], att4[j, 0])
            for y in range(1, NY):
                tot += nt(g4[y, rows, :], att4[j, y])
            yt[j, pl.ds(2 * i, 2)] = (tot * norm).astype(BF).reshape(2, ROWS, BLK)
            return 0

        lax.fori_loop(0, NZ // 2, slab, 0)
        send(yt.at[j, zid(4 * g)], za.at[j, 0], sem_zs.at[j, 0], sem_zr.at[j, 0], dp_dev(0, g))
        send(yt.at[j, zid(-3 * g)], zb.at[j, 0], sem_zs.at[j, 4], sem_zr.at[j, 4], dp_dev(0, -g))

    def mine4(t, lo=0, n=ROWS):
        return pl.ds(pl.multiple_of(t * ROWS + lo, 16), n)

    def chunk(y):
        return gt.at[pl.ds(pl.multiple_of(y * SLAB + tp * ROWS, 16), ROWS)]

    def g4_start():
        for k in range(1, NY):
            y = lax.rem(my_y + k, NY)
            send(chunk(y), g4.at[my_y, mine4(tp)], sem_4s.at[8], sem_4r.at[8], y * NZ + my_z)
        g4[my_y, mine4(tp)] = chunk(my_y)[...]

    def three(sem):
        ref = g4.at[pl.ds(0, NY - 1), pl.ds(0, ROWS)]
        pltpu.make_async_copy(ref, ref, sem).wait()

    def ring4(idx, t, lo, n, dev):
        ref = g4.at[:, mine4(t, lo, n)]
        pltpu.make_async_remote_copy(
            src_ref=ref, dst_ref=ref, send_sem=sem_4s.at[idx], recv_sem=sem_4r.at[idx],
            device_id={"tensor": dev}, device_id_type=MESH,
        ).start()

    def got4(idx, t, lo, n):
        landed(g4.at[:, mine4(t, lo, n)], sem_4r.at[idx])

    hop = ROWS // 2

    def g4_one():
        three(sem_4r.at[8])
        ring4(0, tp, 0, ROWS, right)
        ring4(1, tp, 0, ROWS, left)
        ring4(2, tp, 0, ROWS, twin)

    def g4_two():
        got4(0, left, 0, ROWS)
        ring4(3, left, 0, hop, right)
        ring4(4, left, 0, ROWS, twin)
        got4(1, right, 0, ROWS)
        ring4(5, right, hop, hop, left)
        ring4(6, right, 0, ROWS, twin)

    def g4_three():
        got4(3, far, 0, hop)
        got4(5, far, hop, hop)
        ring4(7, far, 0, ROWS, twin)

    def g4_four():
        got4(2, x_dev(0, 1 - core), 0, ROWS)
        got4(4, x_dev(-1, 1 - core), 0, ROWS)
        got4(6, x_dev(1, 1 - core), 0, ROWS)
        got4(7, x_dev(2, 1 - core), 0, ROWS)

    def z_next(j, s):
        g = sgn(j)
        landed(za.at[j, s], sem_zr.at[j, s])
        if s < 3:
            za[j, s] = (za[j, s].astype(F32) + yt[j, zid((3 - s) * g)].astype(F32)).astype(BF)
            send(za.at[j, s], za.at[j, s + 1], sem_zs.at[j, s + 1], sem_zr.at[j, s + 1], dp_dev(0, g))
        if s < 3:
            landed(zb.at[j, s], sem_zr.at[j, 4 + s])
        if s < 2:
            zb[j, s] = (zb[j, s].astype(F32) + yt[j, zid((s - 2) * g)].astype(F32)).astype(BF)
            send(zb.at[j, s], zb.at[j, s + 1], sem_zs.at[j, 5 + s], sem_zr.at[j, 5 + s], dp_dev(0, -g))
        if s == 3:
            cols = pl.ds(pl.multiple_of(j * BLK, BLK), BLK)
            wg_ref[:, cols] = za[j, 3].astype(F32) + zb[j, 2].astype(F32) + yt[j, my_z].astype(F32)

    def push_back(j, lo=1, hi=NDP):
        exchange(back.at[j], home.at[j], sem_bs.at[j], sem_br.at[j], lo, hi)

    def step(j, _):
        drain(recv_x.at[j], sem_xr.at[j])
        head_block(j)
        back[j] = nt(sel_rt[...], dqt[...]).astype(BF)
        @pl.when((j >= 1) & (j < 3))
        def _():
            a_next(j - 1)

        pl.when(j == 0)(g4_one)
        pl.when(j == 1)(g4_two)
        pl.when(j == 2)(g4_three)

        @pl.when(j >= 2)
        def _():
            push_back(j - 2)

        return 0

    g4_start()
    lax.fori_loop(0, NB, step, 0)

    lane = lax.broadcasted_iota(jnp.int32, (TOK, 2 * HEAD_DIM), 1)
    dkv_h = (dkv[...] * jnp.where(lane < HEAD_DIM, inv, 1.0)).astype(BF)
    back[NB] = nn(sel_rt[...], dkv_h).astype(BF)

    sel_r[...] = (slot_cols == column(ss_row)).astype(BF)
    def settle(j):
        drain(home.at[j], sem_br.at[j])
        return nn(sel_r[...], home[j]).astype(BF)

    g4_four()
    a_end(0)
    a_next(2)
    a_end(1)
    push_back(2, 1, NDP // 2)
    z_next(0, 0)
    z_next(1, 0)
    push_back(2, NDP // 2, NDP)
    a_next(3)
    z_next(0, 1)
    z_next(1, 1)
    a_end(2)
    push_back(3, 1, NDP // 2)
    z_next(0, 2)
    z_next(1, 2)
    z_next(2, 0)
    a_end(3)
    push_back(3, NDP // 2, NDP)
    z_next(0, 3)
    z_next(1, 3)
    z_next(2, 1)
    z_next(3, 0)
    push_back(NB)
    z_next(2, 2)
    z_next(3, 1)
    z_next(2, 3)
    z_next(3, 2)
    z_next(3, 3)
    for j in range(NB):
        qg_ref[:, j * BLK:(j + 1) * BLK] = settle(j)
    got = settle(NB)
    kg_ref[...] = got[:, :HEAD_DIM]
    vg_ref[...] = got[:, HEAD_DIM:]

    drain(send_g, sem_gs)

    def sent(j, _):
        drain(send_x.at[j], sem_xs.at[j])
        drain(back.at[j], sem_bs.at[j])
        return 0

    lax.fori_loop(0, NB + 1, sent, 0)
    for c in cps:
        c.wait_send()

    def ring_sent(j, _):
        landed(att4.at[j, 0], sem_ys.at[j, 0])
        landed(att4.at[j, 0], sem_ys.at[j, 1])
        landed(att4.at[j, 0].at[low], sem_ys.at[j, 2])
        landed(att4.at[j, 0].at[low], sem_ys.at[j, 3])
        for s in range(7):
            landed(za.at[j, 0], sem_zs.at[j, s])
        return 0

    lax.fori_loop(0, NB, ring_sent, 0)
    three(sem_4s.at[8])
    for i in range(8):
        landed(g4.at[:, mine4(0, 0, hop if i in (3, 5) else ROWS)], sem_4s.at[i])


def hand_on(*refs):
    for src, dst in zip(refs[:4], refs[4:]):
        dst[...] = src[...]


def shards(queries, keys, values, out_grad, out_weight, send_slot, recv_index, packed_doc):
    row = lambda a: a.reshape(1, TOK)
    vmem = pl.BlockSpec(memory_space=pltpu.VMEM)
    hbm = pl.BlockSpec(memory_space=pl.ANY)
    dma = pltpu.SemaphoreType.DMA
    grads = pl.pallas_call(
        kernel,
        out_shape=(
            jax.ShapeDtypeStruct((TOK, NB * BLK), BF),
            jax.ShapeDtypeStruct((TOK, HEAD_DIM), BF),
            jax.ShapeDtypeStruct((TOK, HEAD_DIM), BF),
            jax.ShapeDtypeStruct((ROWS, NB * BLK), F32),
        ),
        in_specs=[hbm, hbm, hbm, vmem, hbm, vmem, vmem, vmem],
        out_specs=(vmem,) * 4,
        scratch_shapes=[
            pltpu.VMEM((TOK, NB * BLK), BF),
            pltpu.VMEM((TOK, HEAD_DIM), BF),
            pltpu.VMEM((TOK, HEAD_DIM), BF),
            pltpu.VMEM((NB * BLK, FEAT), BF),
            dma((4,)),
            pltpu.VMEM((LANES, PART), BF),
            pltpu.VMEM((LANES, PART), BF),
            pltpu.VMEM((NB + 1, LANES, BLK), BF),
            pltpu.VMEM((NB + 1, LANES, BLK), BF),
            pltpu.VMEM((NB + 1, LANES, BLK), BF),
            pltpu.VMEM((NB + 1, LANES, BLK), BF),
            pltpu.VMEM((TOK, LANES), BF),
            pltpu.VMEM((LANES, TOK), BF),
            pltpu.VMEM((FEAT, TOK), BF),
            pltpu.VMEM((TOK, TOK), F32),
            pltpu.VMEM((TOK, BLK), BF),
            pltpu.VMEM((BLK, TOK), BF),
            pltpu.VMEM((TOK, BLK), F32),
            pltpu.VMEM((BLK, TOK), BF),
            pltpu.VMEM((BLK, TOK), BF),
            pltpu.VMEM((2, 2, TOK, HALF), F32),
            pltpu.VMEM((NY, SLAB, TOK), BF),
            pltpu.VMEM((NB, NY, BLK, TOK), BF),
            pltpu.VMEM((NB, NZ, ROWS, BLK), BF),
            pltpu.VMEM((NB, 4, ROWS, BLK), BF),
            pltpu.VMEM((NB, 3, ROWS, BLK), BF),
            dma, dma,
            dma((NB + 1,)), dma((NB + 1,)),
            dma((NB + 1,)), dma((NB + 1,)),
            dma((8,)), dma((8,)),
            dma((NB, 4)), dma((NB, 4)),
            dma((NB, 7)), dma((NB, 7)),
            dma((9,)), dma((9,)),
        ],
        compiler_params=pltpu.CompilerParams(
            collective_id=1, has_side_effects=True, vmem_limit_bytes=60 << 20
        ),
        name="packed_attention_backward",
    )(
        queries, keys, values, out_grad, out_weight,
        row(send_slot), row(recv_index), row(packed_doc),
    )
    return pl.pallas_call(
        hand_on,
        out_shape=tuple(jax.ShapeDtypeStruct(a.shape, a.dtype) for a in grads),
        in_specs=[vmem] * 4,
        out_specs=(vmem,) * 4,
        name="results",
    )(*grads)


def solution(mesh):
    both = P("dp", "tensor")
    return jax.shard_map(
        shards,
        mesh=mesh,
        in_specs=(both, both, both, both, P("tensor", None), P("dp"), P("dp"), P("dp")),
        out_specs=(both, both, both, both),
        check_vma=False,
    )
```

```python
import functools
import math

import jax
import jax.numpy as jnp
from jax import lax
from jax.experimental import pallas as pl
from jax.experimental.pallas import tpu as pltpu
from jax.sharding import PartitionSpec as P

MESH = pl.DeviceIdType.MESH
BF = jnp.bfloat16
F32 = jnp.float32
CAP = 32
HEAD_DIM = 128
NY = 4
NZ = 8
NX = 4
NDP = NY * NZ
TOK = 512
LANES = NDP * CAP
BLK = 256
NB = 4
PART = 384
FEAT = 3072
ROWS = FEAT // NDP
SLAB = NZ * ROWS
HALF = TOK // 2


def nn(a, b):
    return lax.dot_general(a, b, (((1,), (0,)), ((), ())), preferred_element_type=F32)


def nt(a, b):
    return lax.dot_general(a, b, (((1,), (1,)), ((), ())), preferred_element_type=F32)


def column(row_ref):
    return jnp.broadcast_to(row_ref[...], (HEAD_DIM, TOK)).T[:, :1]


def kernel(
    q_hbm, k_hbm, v_hbm, g_ref, w_hbm, ss_row, ri_row, doc_row,
    qg_ref, kg_ref, vg_ref, wg_ref,
    q_ref, k_ref, v_ref, w_ref, sem_in,
    send_g, recv_g, send_x, recv_x, back, home,
    sel_r, sel_rt, gt, bias, kv, kvt, dkv, hgt, dqt,
    weights, g4, att4, yt, za, zb,
    sem_gs, sem_gr, sem_xs, sem_xr, sem_bs, sem_br, sem_as, sem_ar, sem_ys, sem_yr, sem_zs, sem_zr,
    sem_4s, sem_4r,
):
    me = lax.axis_index("dp")
    tp = lax.axis_index("tensor")
    my_y, my_z = me // NZ, lax.rem(me, NZ)
    my_x, core = tp // 2, lax.rem(tp, 2)

    def peer(k):
        return lax.rem(my_y + k // NZ, NY) * NZ + lax.rem(my_z + 3 * k, NZ)

    def x_dev(dx, c):
        return lax.rem(my_x + dx + NX, NX) * 2 + c

    def dp_dev(dy, dz):
        return lax.rem(my_y + dy + NY, NY) * NZ + lax.rem(my_z + dz + NZ, NZ)

    loads = [
        pltpu.make_async_copy(src, dst, sem_in.at[i])
        for i, (src, dst) in enumerate(
            ((k_hbm, k_ref), (v_hbm, v_ref), (q_hbm, q_ref), (w_hbm, w_ref))
        )
    ]
    for c in loads:
        c.start()

    barrier = pltpu.get_barrier_semaphore()

    def greet(k, _):
        pl.semaphore_signal(barrier, inc=1, device_id={"dp": peer(k)}, device_id_type=MESH)
        return 0

    lax.fori_loop(1, NDP, greet, 0)
    for t in (x_dev(1, core), x_dev(-1, core), x_dev(0, 1 - core)):
        pl.semaphore_signal(barrier, inc=1, device_id={"tensor": t}, device_id_type=MESH)

    slot_rows = lax.broadcasted_iota(jnp.int32, (LANES, TOK), 0)
    sel_rt[...] = (slot_rows == ss_row[...]).astype(BF)
    send_g[...] = nn(sel_rt[...], g_ref[...]).astype(BF)
    pl.semaphore_wait(barrier, NDP - 1 + 3)

    def rows_of(d):
        return pl.ds(pl.multiple_of(d * CAP, CAP), CAP)

    def exchange(src, dst, s_sem, r_sem, lo=1, hi=NDP):
        def one(k, _):
            d = peer(k)
            pltpu.make_async_remote_copy(
                src_ref=src.at[rows_of(d)], dst_ref=dst.at[rows_of(me)],
                send_sem=s_sem, recv_sem=r_sem, device_id={"dp": d}, device_id_type=MESH,
            ).start()
            return 0

        lax.fori_loop(lo, hi, one, 0)
        if lo == 1:
            dst[rows_of(me)] = src[rows_of(me)]

    def drain(ref, sem):
        whole = ref.at[pl.ds(0, LANES - CAP)]
        pltpu.make_async_copy(whole, whole, sem).wait()

    exchange(send_g, recv_g, sem_gs, sem_gr)
    loads[0].wait()
    loads[1].wait()
    kv_in = jnp.concatenate([k_ref[...], v_ref[...]], axis=1)
    send_x[NB] = nn(sel_rt[...], kv_in).astype(BF)
    exchange(send_x.at[NB], recv_x.at[NB], sem_xs.at[NB], sem_xr.at[NB])

    def push_q(j, _):
        cols = pl.ds(pl.multiple_of(j * BLK, BLK), BLK)
        send_x[j] = nn(sel_rt[...], q_ref[:, cols]).astype(BF)
        exchange(send_x.at[j], recv_x.at[j], sem_xs.at[j], sem_xr.at[j])
        return 0

    loads[2].wait()
    lax.fori_loop(0, NB, push_q, 0)

    slot_cols = lax.broadcasted_iota(jnp.int32, (TOK, LANES), 1)
    sel_r[...] = (slot_cols == column(ri_row)).astype(BF)
    sel_rt[...] = (slot_rows == ri_row[...]).astype(BF)
    key_at = lax.broadcasted_iota(jnp.int32, (TOK, TOK), 0)
    query_at = lax.broadcasted_iota(jnp.int32, (TOK, TOK), 1)
    seen = (column(doc_row) == doc_row[...]) & (key_at <= query_at)
    bias[...] = jnp.where(seen, 0.0, -1e30).astype(F32)
    dkv[...] = jnp.zeros_like(dkv)

    drain(recv_g, sem_gr)

    def feats(t, lo=0, n=PART):
        return pl.ds(pl.multiple_of(t * PART + lo, 16), n)

    mine = nn(sel_r[...], recv_g[...]).T.astype(BF)
    gt[feats(tp)] = mine

    def ring(idx, t, lo, n, dev):
        c = pltpu.make_async_remote_copy(
            src_ref=gt.at[feats(t, lo, n)], dst_ref=gt.at[feats(t, lo, n)],
            send_sem=sem_as.at[idx], recv_sem=sem_ar.at[idx],
            device_id={"tensor": dev}, device_id_type=MESH,
        )
        c.start()
        return c

    right, left, twin = x_dev(1, core), x_dev(-1, core), x_dev(0, 1 - core)
    far = x_dev(2, core)
    half = PART // 2
    cps = [
        ring(0, tp, 0, PART, right),
        ring(1, tp, 0, PART, left),
        ring(2, tp, 0, PART, twin),
    ]

    def arrived(idx, t, lo, n):
        ref = gt.at[feats(t, lo, n)]
        pltpu.make_async_copy(ref, ref, sem_ar.at[idx]).wait()

    arrived(0, left, 0, PART)
    cps.append(ring(3, left, 0, half, right))
    cps.append(ring(4, left, 0, PART, twin))
    arrived(1, right, 0, PART)
    cps.append(ring(5, right, half, half, left))
    cps.append(ring(6, right, 0, PART, twin))
    arrived(3, far, 0, half)
    arrived(5, far, half, half)
    cps.append(ring(7, far, 0, PART, twin))

    drain(recv_x.at[NB], sem_xr.at[NB])
    kv_f = nn(sel_r[...], recv_x[NB])
    kv[...] = kv_f.astype(BF)
    kvt[...] = kv_f.T.astype(BF)

    arrived(2, x_dev(0, 1 - core), 0, PART)
    arrived(4, x_dev(-1, 1 - core), 0, PART)
    arrived(6, x_dev(1, 1 - core), 0, PART)
    arrived(7, x_dev(2, 1 - core), 0, PART)

    loads[3].wait()
    inv = 1.0 / math.sqrt(HEAD_DIM)
    norm = 1.0 / math.sqrt(TOK * NDP)

    def head_block(j):
        rows = pl.ds(pl.multiple_of(j * BLK, BLK), BLK)
        qp = nn(sel_r[...], recv_x[j]).astype(BF)
        places = [(h, b) for h in range(2) for b in range(2)]

        def cut(h, b):
            kn = HALF * (b + 1)
            return kn, slice(h * HEAD_DIM, (h + 1) * HEAD_DIM), slice(b * HALF, (b + 1) * HALF)

        for h, b in places:
            kn, hs, ps = cut(h, b)
            s = nt(kv[:kn, :HEAD_DIM], qp[ps, hs]) + bias[:kn, ps]
            top = jnp.max(s, axis=0, keepdims=True)
            e = jnp.exp((s - top) * inv)
            soft = e * (1.0 / jnp.sum(e, axis=0, keepdims=True))
            weights[h, b, :kn] = soft
            att4[j, my_y, hs, ps] = nn(kvt[HEAD_DIM:, :kn], soft.astype(BF)).astype(BF)

        a_start(j)
        hgt[...] = nn(w_ref[rows, :], gt[...]).astype(BF)
        for h, b in places:
            kn, hs, ps = cut(h, b)
            soft = weights[h, b, :kn]
            hg = hgt[hs, ps]
            dp_ = nn(kv[:kn, HEAD_DIM:], hg)
            inner = jnp.sum(soft * dp_, axis=0, keepdims=True)
            ds = (soft * (dp_ - inner)).astype(BF)
            dqt[hs, ps] = (nn(kvt[:HEAD_DIM, :kn], ds) * inv).astype(BF)
            dkv[:kn, :HEAD_DIM] += nn(ds, qp[ps, hs])
            dkv[:kn, HEAD_DIM:] += nt(soft.astype(BF), hg)

    def yid(k):
        return lax.rem(my_y + k + 2 * NY, NY)

    def zid(k):
        return lax.rem(my_z + k + 2 * NZ, NZ)

    def send(src, dst, ss, rs, dev):
        pltpu.make_async_remote_copy(
            src_ref=src, dst_ref=dst, send_sem=ss, recv_sem=rs,
            device_id={"dp": dev}, device_id_type=MESH,
        ).start()

    def landed(ref, sem):
        pltpu.make_async_copy(ref, ref, sem).wait()

    def sgn(j):
        return 1 - 2 * lax.rem(j, 2)

    def a_start(j):
        mine_ = att4.at[j, my_y]
        send(mine_, mine_, sem_ys.at[j, 0], sem_yr.at[j, 0], dp_dev(1, 0))
        send(mine_, mine_, sem_ys.at[j, 1], sem_yr.at[j, 1], dp_dev(-1, 0))

    low, high = pl.ds(0, BLK // 2), pl.ds(BLK // 2, BLK // 2)

    def a_next(j):
        below, above = att4.at[j, yid(-1)], att4.at[j, yid(1)]
        landed(below, sem_yr.at[j, 0])
        send(below.at[low], below.at[low], sem_ys.at[j, 2], sem_yr.at[j, 2], dp_dev(1, 0))
        landed(above, sem_yr.at[j, 1])
        send(above.at[high], above.at[high], sem_ys.at[j, 3], sem_yr.at[j, 3], dp_dev(-1, 0))

    def a_end(j):
        g = sgn(j)
        opposite = att4.at[j, yid(2)]
        landed(opposite.at[low], sem_yr.at[j, 2])
        landed(opposite.at[high], sem_yr.at[j, 3])

        def slab(i, _):
            rows = pl.ds(pl.multiple_of(i * 2 * ROWS, 2 * ROWS), 2 * ROWS)
            tot = nt(g4[0, rows, :], att4[j, 0])
            for y in range(1, NY):
                tot += nt(g4[y, rows, :], att4[j, y])
            yt[j, pl.ds(2 * i, 2)] = (tot * norm).astype(BF).reshape(2, ROWS, BLK)
            return 0

        lax.fori_loop(0, NZ // 2, slab, 0)
        send(yt.at[j, zid(4 * g)], za.at[j, 0], sem_zs.at[j, 0], sem_zr.at[j, 0], dp_dev(0, g))
        send(yt.at[j, zid(-3 * g)], zb.at[j, 0], sem_zs.at[j, 4], sem_zr.at[j, 4], dp_dev(0, -g))

    def mine4(t, lo=0, n=ROWS):
        return pl.ds(pl.multiple_of(t * ROWS + lo, 16), n)

    def chunk(y):
        return gt.at[pl.ds(pl.multiple_of(y * SLAB + tp * ROWS, 16), ROWS)]

    def g4_start():
        for k in range(1, NY):
            y = lax.rem(my_y + k, NY)
            send(chunk(y), g4.at[my_y, mine4(tp)], sem_4s.at[8], sem_4r.at[8], y * NZ + my_z)
        g4[my_y, mine4(tp)] = chunk(my_y)[...]

    def three(sem):
        ref = g4.at[pl.ds(0, NY - 1), pl.ds(0, ROWS)]
        pltpu.make_async_copy(ref, ref, sem).wait()

    def ring4(idx, t, lo, n, dev):
        ref = g4.at[:, mine4(t, lo, n)]
        pltpu.make_async_remote_copy(
            src_ref=ref, dst_ref=ref, send_sem=sem_4s.at[idx], recv_sem=sem_4r.at[idx],
            device_id={"tensor": dev}, device_id_type=MESH,
        ).start()

    def got4(idx, t, lo, n):
        landed(g4.at[:, mine4(t, lo, n)], sem_4r.at[idx])

    hop = ROWS // 2

    def g4_one():
        three(sem_4r.at[8])
        ring4(0, tp, 0, ROWS, right)
        ring4(1, tp, 0, ROWS, left)
        ring4(2, tp, 0, ROWS, twin)

    def g4_two():
        got4(0, left, 0, ROWS)
        ring4(3, left, 0, hop, right)
        ring4(4, left, 0, ROWS, twin)
        got4(1, right, 0, ROWS)
        ring4(5, right, hop, hop, left)
        ring4(6, right, 0, ROWS, twin)

    def g4_three():
        got4(3, far, 0, hop)
        got4(5, far, hop, hop)
        ring4(7, far, 0, ROWS, twin)

    def g4_four():
        got4(2, x_dev(0, 1 - core), 0, ROWS)
        got4(4, x_dev(-1, 1 - core), 0, ROWS)
        got4(6, x_dev(1, 1 - core), 0, ROWS)
        got4(7, x_dev(2, 1 - core), 0, ROWS)

    def z_next(j, s):
        g = sgn(j)
        landed(za.at[j, s], sem_zr.at[j, s])
        if s < 3:
            za[j, s] = (za[j, s].astype(F32) + yt[j, zid((3 - s) * g)].astype(F32)).astype(BF)
            send(za.at[j, s], za.at[j, s + 1], sem_zs.at[j, s + 1], sem_zr.at[j, s + 1], dp_dev(0, g))
        if s < 3:
            landed(zb.at[j, s], sem_zr.at[j, 4 + s])
        if s < 2:
            zb[j, s] = (zb[j, s].astype(F32) + yt[j, zid((s - 2) * g)].astype(F32)).astype(BF)
            send(zb.at[j, s], zb.at[j, s + 1], sem_zs.at[j, 5 + s], sem_zr.at[j, 5 + s], dp_dev(0, -g))
        if s == 3:
            cols = pl.ds(pl.multiple_of(j * BLK, BLK), BLK)
            wg_ref[:, cols] = za[j, 3].astype(F32) + zb[j, 2].astype(F32) + yt[j, my_z].astype(F32)

    def push_back(j, lo=1, hi=NDP):
        exchange(back.at[j], home.at[j], sem_bs.at[j], sem_br.at[j], lo, hi)

    def step(j, _):
        drain(recv_x.at[j], sem_xr.at[j])
        head_block(j)
        back[j] = nt(sel_rt[...], dqt[...]).astype(BF)
        @pl.when((j >= 1) & (j < 3))
        def _():
            a_next(j - 1)

        pl.when(j == 0)(g4_one)
        pl.when(j == 1)(g4_two)
        pl.when(j == 2)(g4_three)

        @pl.when(j >= 2)
        def _():
            push_back(j - 2)

        return 0

    g4_start()
    lax.fori_loop(0, NB, step, 0)

    lane = lax.broadcasted_iota(jnp.int32, (TOK, 2 * HEAD_DIM), 1)
    dkv_h = (dkv[...] * jnp.where(lane < HEAD_DIM, inv, 1.0)).astype(BF)
    back[NB] = nn(sel_rt[...], dkv_h).astype(BF)

    sel_r[...] = (slot_cols == column(ss_row)).astype(BF)
    def settle(j):
        drain(home.at[j], sem_br.at[j])
        return nn(sel_r[...], home[j]).astype(BF)

    g4_four()
    a_end(0)
    a_next(2)
    a_end(1)
    push_back(2, 1, NDP // 2)
    z_next(0, 0)
    z_next(1, 0)
    push_back(2, NDP // 2, NDP)
    a_next(3)
    z_next(0, 1)
    z_next(1, 1)
    a_end(2)
    push_back(3, 1, NDP // 2)
    z_next(0, 2)
    z_next(1, 2)
    z_next(2, 0)
    a_end(3)
    push_back(3, NDP // 2, NDP)
    z_next(0, 3)
    z_next(1, 3)
    z_next(2, 1)
    qg_ref[:, 0 * BLK:1 * BLK] = settle(0)
    z_next(3, 0)
    z_next(2, 2)
    qg_ref[:, 1 * BLK:2 * BLK] = settle(1)
    z_next(3, 1)
    push_back(NB)
    z_next(2, 3)
    qg_ref[:, 2 * BLK:3 * BLK] = settle(2)
    z_next(3, 2)
    z_next(3, 3)
    for j in range(3, NB):
        qg_ref[:, j * BLK:(j + 1) * BLK] = settle(j)
    got = settle(NB)
    kg_ref[...] = got[:, :HEAD_DIM]
    vg_ref[...] = got[:, HEAD_DIM:]

    drain(send_g, sem_gs)

    def sent(j, _):
        drain(send_x.at[j], sem_xs.at[j])
        drain(back.at[j], sem_bs.at[j])
        return 0

    lax.fori_loop(0, NB + 1, sent, 0)
    for c in cps:
        c.wait_send()

    def ring_sent(j, _):
        landed(att4.at[j, 0], sem_ys.at[j, 0])
        landed(att4.at[j, 0], sem_ys.at[j, 1])
        landed(att4.at[j, 0].at[low], sem_ys.at[j, 2])
        landed(att4.at[j, 0].at[low], sem_ys.at[j, 3])
        for s in range(7):
            landed(za.at[j, 0], sem_zs.at[j, s])
        return 0

    lax.fori_loop(0, NB, ring_sent, 0)
    three(sem_4s.at[8])
    for i in range(8):
        landed(g4.at[:, mine4(0, 0, hop if i in (3, 5) else ROWS)], sem_4s.at[i])


def hand_on(*refs):
    for src, dst in zip(refs[:4], refs[4:]):
        dst[...] = src[...]


def shards(queries, keys, values, out_grad, out_weight, send_slot, recv_index, packed_doc):
    row = lambda a: a.reshape(1, TOK)
    vmem = pl.BlockSpec(memory_space=pltpu.VMEM)
    hbm = pl.BlockSpec(memory_space=pl.ANY)
    dma = pltpu.SemaphoreType.DMA
    grads = pl.pallas_call(
        kernel,
        out_shape=(
            jax.ShapeDtypeStruct((TOK, NB * BLK), BF),
            jax.ShapeDtypeStruct((TOK, HEAD_DIM), BF),
            jax.ShapeDtypeStruct((TOK, HEAD_DIM), BF),
            jax.ShapeDtypeStruct((ROWS, NB * BLK), F32),
        ),
        in_specs=[hbm, hbm, hbm, vmem, hbm, vmem, vmem, vmem],
        out_specs=(vmem,) * 4,
        scratch_shapes=[
            pltpu.VMEM((TOK, NB * BLK), BF),
            pltpu.VMEM((TOK, HEAD_DIM), BF),
            pltpu.VMEM((TOK, HEAD_DIM), BF),
            pltpu.VMEM((NB * BLK, FEAT), BF),
            dma((4,)),
            pltpu.VMEM((LANES, PART), BF),
            pltpu.VMEM((LANES, PART), BF),
            pltpu.VMEM((NB + 1, LANES, BLK), BF),
            pltpu.VMEM((NB + 1, LANES, BLK), BF),
            pltpu.VMEM((NB + 1, LANES, BLK), BF),
            pltpu.VMEM((NB + 1, LANES, BLK), BF),
            pltpu.VMEM((TOK, LANES), BF),
            pltpu.VMEM((LANES, TOK), BF),
            pltpu.VMEM((FEAT, TOK), BF),
            pltpu.VMEM((TOK, TOK), F32),
            pltpu.VMEM((TOK, BLK), BF),
            pltpu.VMEM((BLK, TOK), BF),
            pltpu.VMEM((TOK, BLK), F32),
            pltpu.VMEM((BLK, TOK), BF),
            pltpu.VMEM((BLK, TOK), BF),
            pltpu.VMEM((2, 2, TOK, HALF), F32),
            pltpu.VMEM((NY, SLAB, TOK), BF),
            pltpu.VMEM((NB, NY, BLK, TOK), BF),
            pltpu.VMEM((NB, NZ, ROWS, BLK), BF),
            pltpu.VMEM((NB, 4, ROWS, BLK), BF),
            pltpu.VMEM((NB, 3, ROWS, BLK), BF),
            dma, dma,
            dma((NB + 1,)), dma((NB + 1,)),
            dma((NB + 1,)), dma((NB + 1,)),
            dma((8,)), dma((8,)),
            dma((NB, 4)), dma((NB, 4)),
            dma((NB, 7)), dma((NB, 7)),
            dma((9,)), dma((9,)),
        ],
        compiler_params=pltpu.CompilerParams(
            collective_id=1, has_side_effects=True, vmem_limit_bytes=60 << 20
        ),
        name="packed_attention_backward",
    )(
        queries, keys, values, out_grad, out_weight,
        row(send_slot), row(recv_index), row(packed_doc),
    )
    return pl.pallas_call(
        hand_on,
        out_shape=tuple(jax.ShapeDtypeStruct(a.shape, a.dtype) for a in grads),
        in_specs=[vmem] * 4,
        out_specs=(vmem,) * 4,
        name="results",
    )(*grads)


def solution(mesh):
    both = P("dp", "tensor")
    return jax.shard_map(
        shards,
        mesh=mesh,
        in_specs=(both, both, both, both, P("tensor", None), P("dp"), P("dp"), P("dp")),
        out_specs=(both, both, both, both),
        check_vma=False,
    )
```
